32 devices in a mesh: section: 4 (over z), head: 2 (over y), blk: 4 (over x, core).
Axes of the slice: x: 2, y: 2, z: 4, core: 2. Of those that a mesh axis runs over, the one named last changes fastest.
Arguments:
- query_states: bfloat16 [4, 3072, 4096], P('section', 'blk', 'head'), may hold values from -8 to 8
- key_states: bfloat16 [4, 3072, 4096], P('section', 'blk', 'head'), may hold values from -8 to 8
- value_states: bfloat16 [4, 3072, 4096], P('section', 'blk', 'head'), may hold values from -6 to 6
- grad_next: bfloat16 [4, 3072, 4096], P('section', ('blk', 'head')), may hold values from -332 to 332
- valid_count: int32 [4], P('section'), may hold values from 768 to 3072, as said below
Outputs:
- grad_query: bfloat16 [4, 3072, 4096], P('section', ('blk', 'head'))
- grad_key: bfloat16 [4, 3072, 4096], P('section', ('blk', 'head'))
- grad_value: bfloat16 [4, 3072, 4096], P('section', ('blk', 'head'))
The draws below stay inside these ranges and needn't reach their ends.
Inputs may be any that keep to these rules, and one draw needn't show every extreme that they name: The live tokens of a window are its first valid_count[s] slots; in every draw some section's window is full.
All inputs are finite; a program needn't handle non-finite values.
Results may differ from the reference program's by a relative error of at most 0.01.
Values may be sent and summed in bfloat16 or wider, within the bound.
No kernel may reach another device: no remote copies, remote signals or barrier semaphores. Data moves between devices by JAX's collectives and lax.ppermute only.
A program may use at most 192 MiB of HBM per device.

```python
import jax
import jax.numpy as jnp
from jax import lax

HEADS = 32
HD = 128
SECTIONS = 4
SEQ = 3072


def base_field(key, salt):
    shape = (SECTIONS, SEQ, HEADS * HD)
    return jax.random.truncated_normal(jax.random.fold_in(key, salt), -6.0, 6.0, shape, jnp.float32)


def draw_query_states(key, part):
    field = base_field(key, 1)
    return field.astype(jnp.bfloat16)


def draw_key_states(key, part):
    field = base_field(key, 2)
    return field.astype(jnp.bfloat16)


def draw_valid_count(key, part):
    lengths = jax.random.randint(jax.random.fold_in(key, 8), (SECTIONS,), SEQ // 4, SEQ + 1)
    full_section = jax.random.randint(jax.random.fold_in(key, 9), (), 0, SECTIONS)
    return jnp.where(jnp.arange(SECTIONS) == full_section, SEQ, lengths).astype(jnp.int32)


def level_of(stream_key, extent, pieces, least, top_value):
    loudness, own = 1.0, jax.random.fold_in(stream_key, 6)
    for dim, blocks in pieces:
        steps = jnp.exp(jax.random.uniform(jax.random.fold_in(own, dim), (blocks,), jnp.float32, least / len(pieces), top_value / len(pieces)))
        loudness = loudness * jnp.repeat(steps, extent[dim] // blocks).reshape([-1 if axis == dim else 1 for axis in range(len(extent))])
    return loudness


def scatter_about(key, dims, width, reach, pieces=(), kind=jnp.bfloat16):
    entries = jax.random.normal(key, dims, jnp.float32) * width
    if len(pieces) > 0:
        entries = level_of(key, dims, pieces, -0.22, 0.18) * entries
    return jnp.clip(entries, min=-reach, max=reach).astype(kind)


def setup_inputs(seed: int = 0) -> dict:
    arg_keys = jax.random.split(jax.random.key(seed), 6)
    query_states = draw_query_states(jax.random.fold_in(arg_keys[5], 71), 0)
    key_states = draw_key_states(jax.random.fold_in(arg_keys[5], 71), 0)
    value_states = scatter_about(arg_keys[2], (SECTIONS, SEQ, HEADS * HD), 1.0, 6.0, ((0, 4), (1, 4), (2, 2)))
    grad_next = scatter_about(arg_keys[3], (SECTIONS, SEQ, HEADS * HD), (SEQ ** 0.5), 332.0, ((0, 4), (1, 8)))
    valid_count = draw_valid_count(jax.random.fold_in(arg_keys[5], 71), 0)
    return dict(query_states=query_states, key_states=key_states, value_states=value_states, grad_next=grad_next, valid_count=valid_count)


def head_grads(query_head, key_head, value_head, grad_head, key_live):
    scale = HD ** -0.5
    scores = jnp.dot(query_head, key_head.T, preferred_element_type=jnp.float32) * scale
    scores = jnp.where(key_live[None, :], scores, -jnp.inf)
    row_top = jnp.max(scores, axis=1, keepdims=True)
    log_total = row_top + jnp.log(jnp.sum(jnp.exp(scores - row_top), axis=1, keepdims=True))
    probs = jnp.exp(scores - log_total)
    grad_probs = jnp.dot(grad_head, value_head.T, preferred_element_type=jnp.float32)
    delta = jnp.sum(probs * grad_probs, axis=1, keepdims=True)
    grad_scores = (probs * (grad_probs - delta)).astype(jnp.bfloat16)
    prob_low = probs.astype(jnp.bfloat16)
    grad_value = jnp.dot(prob_low.T, grad_head, preferred_element_type=jnp.float32)
    grad_query = jnp.dot(grad_scores, key_head, preferred_element_type=jnp.float32) * scale
    grad_key = jnp.dot(grad_scores.T, query_head, preferred_element_type=jnp.float32) * scale
    return grad_query.astype(jnp.bfloat16), grad_key.astype(jnp.bfloat16), grad_value.astype(jnp.bfloat16)


def split_heads(matrix):
    return matrix.reshape(SEQ, HEADS, HD).transpose(1, 0, 2)


def join_heads(stacked):
    return stacked.transpose(1, 0, 2).reshape(SEQ, HEADS * HD)


def section_grads(queries, keys_here, values_here, grads, limit):
    positions = jnp.arange(SEQ, dtype=jnp.int32)
    live_rows = positions < limit
    grads = jnp.where(live_rows[:, None], grads, jnp.zeros_like(grads))

    def one_head(parts):
        return head_grads(parts[0], parts[1], parts[2], parts[3], live_rows)

    grad_q, grad_k, grad_v = lax.map(one_head, (split_heads(queries), split_heads(keys_here), split_heads(values_here), split_heads(grads)))
    return join_heads(grad_q), join_heads(grad_k), join_heads(grad_v)


def reference(query_states, key_states, value_states, grad_next, valid_count):
    query_list, key_list, value_list = [], [], []
    for section_index in range(SECTIONS):
        later = (section_index + 1) % SECTIONS
        grad_q, grad_k, grad_v = section_grads(query_states[section_index], key_states[section_index], value_states[section_index], grad_next[later], valid_count[section_index])
        query_list.append(grad_q)
        key_list.append(grad_k)
        value_list.append(grad_v)
    return jnp.stack(query_list), jnp.stack(key_list), jnp.stack(value_list)
```

```python
import functools
import math

import jax
import jax.numpy as jnp
from jax import lax
from jax.experimental import pallas as pl
from jax.experimental.pallas import tpu as pltpu
from jax.sharding import PartitionSpec as P

HD = 128
LOG2E = math.log2(math.e)
MASKED = -1e30
NT = (((1,), (1,)), ((), ()))
MIB = 2**20


def cols(index):
    return pl.ds(pl.multiple_of(index * HD, HD), HD)


def run_copies(pairs, sems):
    copies = [pltpu.make_async_copy(src, dst, sems.at[i]) for i, (src, dst) in enumerate(pairs)]
    for copy in copies:
        copy.start()
    for copy in copies:
        copy.wait()


def run_staged(pairs, stage, sems):
    loads, stores = [], []
    for i, (src, dst) in enumerate(pairs):
        buf = stage.at[i, pl.ds(0, src.shape[0]), :]
        loads.append(pltpu.make_async_copy(src, buf, sems.at[0, i]))
        stores.append(pltpu.make_async_copy(buf, dst, sems.at[1, i]))
    for load in loads:
        load.start()
    for load, store in zip(loads, stores):
        load.wait()
        store.start()
    for store in stores:
        store.wait()


class Chain:
    def __init__(self):
        self.token = jnp.zeros((8, HD), jnp.float32)

    def call(self, body, place, operands, out_shapes, aliases=None, **kwargs):
        any_space = pl.BlockSpec(memory_space=pl.ANY)
        n_in, n_out = len(operands), len(out_shapes)

        def whole(place_ref, *refs):
            body(place_ref, refs[1 : n_in + 1], refs[n_in + 2 : n_in + 2 + n_out], refs[n_in + 2 + n_out :])

        self.token, *outs = pl.pallas_call(
            whole,
            out_shape=(jax.ShapeDtypeStruct(self.token.shape, self.token.dtype), *out_shapes),
            in_specs=[pl.BlockSpec(memory_space=pltpu.SMEM)] + [any_space] * (n_in + 1),
            out_specs=(any_space,) * (n_out + 1),
            input_output_aliases={i + 2: o + 1 for i, o in (aliases or {}).items()},
            **kwargs,
        )(place, self.token, *operands)
        return outs


def copy_kernel(chain, plan, count, rows, out_shapes, place, operands, name, aliases=None):
    def body(place_ref, ins, outs, scratch):
        run_staged(plan(place_ref, ins, outs), *scratch)

    moved = count * rows * HD * 2
    return chain.call(
        body,
        place,
        operands,
        out_shapes,
        aliases,
        scratch_shapes=[
            pltpu.VMEM((count, rows, HD), jnp.bfloat16),
            pltpu.SemaphoreType.DMA((2, count)),
        ],
        compiler_params=pltpu.CompilerParams(vmem_limit_bytes=moved + 4 * MIB),
        cost_estimate=pl.CostEstimate(flops=40_000_000_000, bytes_accessed=1, transcendentals=0),
        name=name,
    )


class Layout:
    def __init__(self, rows, width, nb, nh):
        self.rows, self.nb, self.nh = rows, nb, nh
        self.heads = width // HD
        self.per = self.heads // nb
        self.nx = nb // 2
        self.part = rows // nh
        self.seq = rows * nb


def bf16(*shape):
    return jax.ShapeDtypeStruct(shape, jnp.bfloat16)


def attention_body(lay, bq, tk, place, q_s, k_s, v_s, g_s, dq_s, dk_s, dv_s, e_s, d_s, m_s, kt_s, ak_s, av_s):
    seq, rows = lay.seq, lay.rows
    nq, nt = seq // bq, seq // tk
    c = HD**-0.5 * LOG2E
    limit, blk = place[0], place[1]
    live = [jnp.clip(limit - (blk ^ k) * rows, 0, rows) for k in range(lay.nb)]
    full = limit >= seq

    @pl.when(jnp.logical_not(full))
    def _():
        for k in range(lay.nb):
            span = slice(k * rows, (k + 1) * rows)
            row = lax.broadcasted_iota(jnp.int32, (rows, HD), 0)
            g_s[span, :] = jnp.where(row < live[k], g_s[span, :], jnp.zeros((rows, HD), jnp.bfloat16))

    kt_s[...] = k_s[...].T
    ak_s[...] = jnp.zeros_like(ak_s)
    av_s[...] = jnp.zeros_like(av_s)

    def run(masked):
        def step(i, carry):
            off = pl.multiple_of(i * bq, bq)
            qb = q_s[pl.ds(off, bq), :]
            gb = g_s[pl.ds(off, bq), :]
            top = jnp.full((1, bq), MASKED, jnp.float32)
            total = jnp.zeros((1, bq), jnp.float32)
            dot = total
            for t in range(nt):
                span = slice(t * tk, (t + 1) * tk)
                s = lax.dot_general(k_s[span, :], qb, NT, preferred_element_type=jnp.float32) * c
                if masked:
                    piece, base = t * tk // rows, t * tk % rows
                    row = lax.broadcasted_iota(jnp.int32, (tk, bq), 0)
                    s = jnp.where(row < live[piece] - base, s, MASKED)
                new = jnp.maximum(top, jnp.max(s, axis=0, keepdims=True))
                e = jnp.exp2(s - new)
                d = lax.dot_general(v_s[span, :], gb, NT, preferred_element_type=jnp.float32)
                e_s[span, :] = e
                d_s[span, :] = d
                m_s[t : t + 1, :] = new
                fade = jnp.exp2(top - new)
                total = total * fade + jnp.sum(e, axis=0, keepdims=True)
                dot = dot * fade + jnp.sum(e * d, axis=0, keepdims=True)
                top = new
            delta = dot / total
            lse = top + jnp.log2(total)
            dqt = jnp.zeros((HD, bq), jnp.float32)
            for t in range(nt):
                span = slice(t * tk, (t + 1) * tk)
                p = e_s[span, :] * jnp.exp2(m_s[t : t + 1, :] - lse)
                ds = (p * (d_s[span, :] - delta)).astype(jnp.bfloat16)
                pb = p.astype(jnp.bfloat16)
                av_s[span, :] += jnp.dot(pb, gb, preferred_element_type=jnp.float32)
                ak_s[span, :] += jnp.dot(ds, qb, preferred_element_type=jnp.float32)
                dqt += jnp.dot(kt_s[:, span], ds, preferred_element_type=jnp.float32)
            dq_s[pl.ds(off, bq), :] = (dqt * HD**-0.5).T.astype(jnp.bfloat16)
            return carry

        lax.fori_loop(0, nq, step, 0)

    pl.when(full)(lambda: run(False))
    pl.when(jnp.logical_not(full))(lambda: run(True))
    dk_s[...] = (ak_s[...] * HD**-0.5).astype(jnp.bfloat16)
    dv_s[...] = av_s[...].astype(jnp.bfloat16)


def attention(chain, lay, place, sources, operands, name):
    seq, part = lay.seq, lay.part
    bq, tk = math.gcd(512, seq), math.gcd(256, lay.rows)
    def body(place_ref, ins, outs, scratch):
        bufs, results, work, sems = scratch[:4], scratch[4:7], scratch[7:-1], scratch[-1]
        pairs = [
            (src, buf.at[pl.ds(start, size), :])
            for buf, listing in zip(bufs, sources(place_ref, ins))
            for start, size, src in listing
        ]
        run_copies(pairs, sems)
        attention_body(lay, bq, tk, place_ref, *bufs, *results, *work)
        run_copies(
            [
                (
                    results[t].at[pl.ds((k * lay.nh + h) * part, part), :],
                    outs[0].at[h * lay.nb + (place_ref[1] ^ k), t],
                )
                for h in range(lay.nh)
                for k in range(lay.nb)
                for t in range(3)
            ],
            sems,
        )

    flops = 2 * seq * seq * HD
    vec = lambda *s: pltpu.VMEM(s, jnp.bfloat16)
    acc = lambda *s: pltpu.VMEM(s, jnp.float32)
    n_sems = 4 * lay.nb * lay.nh
    return chain.call(
        body,
        place,
        operands,
        [bf16(lay.nh * lay.nb, 3, part, HD)],
        scratch_shapes=[vec(seq, HD)] * 7
        + [acc(seq, bq), acc(seq, bq), acc(-(-seq // tk // 8) * 8, bq), vec(HD, seq), acc(seq, HD), acc(seq, HD)]
        + [pltpu.SemaphoreType.DMA((n_sems,))],
        compiler_params=pltpu.CompilerParams(vmem_limit_bytes=40 * MIB),
        cost_estimate=pl.CostEstimate(flops=400_000_000_000, bytes_accessed=1, transcendentals=0),
        name=name,
    )


def split_heads_program(lay, query_states, key_states, value_states, grad_next, valid_count, sections):
    nb, nh, nx, per, part, rows, heads = lay.nb, lay.nh, lay.nx, lay.per, lay.part, lay.rows, lay.heads
    blk, head = lax.axis_index("blk"), lax.axis_index("head")
    place = jnp.stack([valid_count[0], blk, head]).astype(jnp.int32)
    qkv = [query_states, key_states, value_states]
    chain = Chain()

    def grad_rows(at, refs, i, dest):
        return [(pl.multiple_of((at[2] ^ kh) * part, part), part, refs[kh].at[i, dest]) for kh in range(nh)]

    def send_grads(group):
        def plan(at, ins, outs):
            pairs = []
            for kh in range(nh):
                for i, c in enumerate(group):
                    for o in range(nb):
                        src = ins[0].at[0, :, cols((at[2] ^ kh) * heads + o * per + c)]
                        pairs.append((src, outs[kh].at[i, o]))
            return pairs

        shape = bf16(len(group), nb, part, HD)
        count = nh * len(group) * nb
        packed = copy_kernel(
            chain, plan, count, part, [shape] * nh, place, [grad_next], f"pack_grads_{group[0]}"
        )
        moved = []
        for kh in range(nh):
            route = [
                (s * nh + h, (s - 1) % sections * nh + (h ^ kh))
                for s in range(sections)
                for h in range(nh)
            ]
            moved.append(lax.ppermute(packed[kh], ("section", "head"), route))
        return {c: (moved, i) for i, c in enumerate(group)}

    def blk_send(x, k):
        return lax.ppermute(x, "blk", [(i, i ^ k) for i in range(nb)])

    def send_far(c, kx, tensors, grads, name):
        refs, slot = grads if grads else ([], 0)
        extra = 1 if grads else 0

        def plan(at, ins, outs):
            pairs = []
            for j in range(2):
                dest = at[1] ^ (2 * kx + j)
                for t in range(len(tensors)):
                    pairs.append((ins[t].at[0, :, cols(dest * per + c)], outs[0].at[t, j]))
                if extra:
                    for start, size, src in grad_rows(at, ins[len(tensors) :], slot, dest):
                        pairs.append((src, outs[0].at[len(tensors), j, pl.ds(start, size), :]))
            return pairs

        n = 2 * (len(tensors) + extra * nh)
        shape = bf16(len(tensors) + extra, 2, rows, HD)
        packed = copy_kernel(chain, plan, n, rows, [shape], place, [*tensors, *refs], name)
        return blk_send(packed[0], 2 * kx)

    def send_near(c, grads, far):
        refs, slot = grads

        def plan(at, ins, outs):
            pairs = []
            dest = at[1] ^ 1
            for t in range(3):
                pairs.append((ins[t].at[0, :, cols(dest * per + c)], outs[0].at[t, 0]))
            for start, size, src in grad_rows(at, ins[3 : 3 + nh], slot, dest):
                pairs.append((src, outs[0].at[3, 0, pl.ds(start, size), :]))
            rest = iter(ins[3 + nh :])
            for kx in range(1, nx):
                for begin, count, _ in far[kx]:
                    ref = next(rest)
                    for t in range(count):
                        pairs.append((ref.at[t, 1], outs[0].at[begin + t, kx]))
            return pairs

        arrays = [a for kx in range(1, nx) for _, _, a in far[kx]]
        n = 3 + nh + 4 * (nx - 1)
        packed = copy_kernel(
            chain, plan, n, rows, [bf16(4, nx, rows, HD)], place, [*qkv, *refs, *arrays], f"pack_near_{c}"
        )
        return blk_send(packed[0], 1)

    def attend(c, grads, far, near):
        refs, slot = grads

        def sources(at, ins):
            near_ref = ins[3 + nh]
            far_refs = iter(ins[4 + nh :])
            listing = [[], [], [], []]
            for t in range(3):
                listing[t].append((0, rows, ins[t].at[0, :, cols(at[1] * per + c)]))
            listing[3].extend(grad_rows(at, ins[3 : 3 + nh], slot, at[1]))
            for kx in range(nx):
                for t in range(4):
                    listing[t].append(((2 * kx + 1) * rows, rows, near_ref.at[t, kx]))
            for kx in range(1, nx):
                for begin, count, _ in far[kx]:
                    ref = next(far_refs)
                    for t in range(count):
                        listing[begin + t].append((2 * kx * rows, rows, ref.at[t, 0]))
            return listing

        arrays = [a for kx in range(1, nx) for _, _, a in far[kx]]
        sent = attention(chain, lay, place, sources, [*qkv, *refs, near, *arrays], f"attention_{c}")
        return lax.all_to_all(sent[0], ("head", "blk"), split_axis=0, concat_axis=0, tiled=True)

    def place_outputs(c, got, outs):
        def plan(at, ins, out_refs):
            return [
                (ins[0].at[h * nb + o, t], out_refs[t].at[0, :, cols(h * heads + o * per + c)])
                for h in range(nh)
                for o in range(nb)
                for t in range(3)
            ]

        shape = bf16(1, part, nh * heads * HD)
        aliases = {1 + t: t for t in range(3)} if outs else None
        operands = [got, *(outs or [])]
        return copy_kernel(
            chain, plan, 3 * nh * nb, part, [shape] * 3, place, operands, f"unpack_{c}", aliases
        )

    fars = range(1, nx)
    far, near, grads, got, outs = {}, {}, {}, {}, None

    def far_tensors(c, tensors, cotangent, first):
        for kx in fars:
            name = f"pack_far_{c}_{kx}_{first}"
            count = len(tensors) + (1 if cotangent else 0)
            x = send_far(c, kx, tensors, grads[c] if cotangent else None, name)
            far.setdefault(c, {}).setdefault(kx, []).append((first, count, x))

    far_tensors(0, qkv, False, 0)
    grads.update(send_grads([0]))
    if per > 1:
        grads.update(send_grads([1]))
    far_tensors(0, [], True, 3)
    if per > 1:
        far_tensors(1, qkv, False, 0)
    near[0] = send_near(0, grads[0], far[0])
    if per > 1:
        far_tensors(1, [], True, 3)
    if per > 2:
        grads.update(send_grads(list(range(2, per))))
        far_tensors(2, qkv, False, 0)
    for c in range(per):
        got[c] = attend(c, grads[c], far[c], near[c])
        if c + 1 < per:
            near[c + 1] = send_near(c + 1, grads[c + 1], far[c + 1])
        if c + 2 < per and c == 0:
            far_tensors(2, [], True, 3)
        if c + 3 < per:
            far_tensors(c + 3, qkv, True, 0)
        if c > 0:
            outs = place_outputs(c - 1, got[c - 1], outs)
    outs = place_outputs(per - 1, got[per - 1], outs)
    return tuple(outs)


def shifted(x, axis, by):
    peers = lax.axis_size(axis)
    return lax.ppermute(x, axis, [(i, (i + by) % peers) for i in range(peers)])


def masked_scores(query_block, key_block, key_positions, limit):
    scores = jnp.einsum(
        "qhd,khd->hqk", query_block, key_block, preferred_element_type=jnp.float32
    ) * HD ** (-0.5)
    return jnp.where(key_positions[None, None, :] < limit, scores, -jnp.inf)


def gathered_program(query_states, key_states, value_states, grad_next, valid_count):
    scale = HD ** (-0.5)
    blk_index = lax.axis_index("blk")
    incoming = shifted(grad_next, "section", -1)
    grads = lax.all_to_all(incoming, "head", split_axis=2, concat_axis=1, tiled=True)
    shard_rows = query_states.shape[1]
    width = query_states.shape[2]
    local_heads = width // HD
    limit = valid_count[0]
    own_positions = blk_index * shard_rows + jnp.arange(shard_rows, dtype=jnp.int32)
    grads = jnp.where((own_positions < limit)[None, :, None], grads, jnp.zeros_like(grads))
    query_heads = query_states[0].reshape(shard_rows, local_heads, HD)
    grad_heads = grads[0].reshape(shard_rows, local_heads, HD)
    gathered_keys, gathered_values = (
        lax.all_gather(key_states, "blk", axis=1, tiled=True),
        lax.all_gather(value_states, "blk", axis=1, tiled=True),
    )
    key_count = gathered_keys.shape[1]
    block_rows = math.gcd(512, key_count)
    block_count = key_count // block_rows
    key_blocks = gathered_keys[0].reshape(block_count, block_rows, local_heads, HD)
    value_blocks = gathered_values[0].reshape(block_count, block_rows, local_heads, HD)
    position_blocks = jnp.arange(key_count, dtype=jnp.int32).reshape(block_count, block_rows)

    def forward_step(carry, block):
        run_max, run_sum, run_dot = carry
        key_block, value_block, key_pos = block
        scores = masked_scores(query_heads, key_block, key_pos, limit)
        grad_probs = jnp.einsum(
            "qhd,khd->hqk", grad_heads, value_block, preferred_element_type=jnp.float32
        )
        new_max = jnp.maximum(run_max, jnp.max(scores, axis=2))
        factor = jnp.exp(run_max - new_max)
        weights = jnp.exp(scores - new_max[:, :, None])
        run_sum = run_sum * factor + jnp.sum(weights, axis=2)
        run_dot = run_dot * factor + jnp.sum(weights * grad_probs, axis=2)
        return ((new_max, run_sum, run_dot), None)

    start_max = jnp.full((local_heads, shard_rows), -jnp.inf, jnp.float32)
    start_zero = jnp.zeros((local_heads, shard_rows), jnp.float32)
    (run_max, run_sum, run_dot), _ = lax.scan(
        forward_step,
        (start_max, start_zero, start_zero),
        (key_blocks, value_blocks, position_blocks),
    )
    log_total = run_max + jnp.log(run_sum)
    delta = run_dot / run_sum

    def block_terms(
        query_block, grad_block, key_block, value_block, key_pos, block_log, block_delta
    ):
        scores = masked_scores(query_block, key_block, key_pos, limit)
        probs = jnp.exp(scores - block_log[:, :, None])
        grad_probs = jnp.einsum(
            "qhd,khd->hqk", grad_block, value_block, preferred_element_type=jnp.float32
        )
        grad_scores = (probs * (grad_probs - block_delta[:, :, None])).astype(jnp.bfloat16)
        return (probs.astype(jnp.bfloat16), grad_scores)

    zero_rows = jnp.zeros((shard_rows, local_heads, HD), jnp.float32)

    def query_step(grad_q, block):
        key_block, value_block, key_pos = block
        prob_low, grad_scores = block_terms(
            query_heads, grad_heads, key_block, value_block, key_pos, log_total, delta
        )
        grad_q = (
            grad_q
            + jnp.einsum("hqk,khd->qhd", grad_scores, key_block, preferred_element_type=jnp.float32)
            * scale
        )
        return (grad_q, None)

    grad_q, _ = lax.scan(query_step, zero_rows, (key_blocks, value_blocks, position_blocks))
    all_log, all_delta = (
        lax.all_gather(log_total.T[None], "blk", axis=1, tiled=True),
        lax.all_gather(delta.T[None], "blk", axis=1, tiled=True),
    )
    key_heads = key_states[0].reshape(shard_rows, local_heads, HD)
    value_heads = value_states[0].reshape(shard_rows, local_heads, HD)
    piece_queries = lax.all_gather(query_states, "blk", axis=1, tiled=True)
    piece_grads = lax.all_gather(grads, "blk", axis=1, tiled=True)
    piece_rows = piece_queries.shape[1]
    sub_rows = math.gcd(shard_rows, piece_rows)
    sub_count = piece_rows // sub_rows
    piece_log = all_log[0]
    piece_delta = all_delta[0]
    sub_queries = piece_queries[0].reshape(sub_count, sub_rows, local_heads, HD)
    sub_grads = piece_grads[0].reshape(sub_count, sub_rows, local_heads, HD)
    sub_log = piece_log.reshape(sub_count, sub_rows, local_heads)
    sub_delta = piece_delta.reshape(sub_count, sub_rows, local_heads)

    def sub_step(accum, sub):
        acc_k, acc_v = accum
        query_block, grad_block, block_log, block_delta = sub
        prob_low, grad_scores = block_terms(
            query_block,
            grad_block,
            key_heads,
            value_heads,
            own_positions,
            block_log.T,
            block_delta.T,
        )
        acc_v = acc_v + jnp.einsum(
            "hqk,qhd->khd", prob_low, grad_block, preferred_element_type=jnp.float32
        )
        acc_k = (
            acc_k
            + jnp.einsum(
                "hqk,qhd->khd", grad_scores, query_block, preferred_element_type=jnp.float32
            )
            * scale
        )
        return ((acc_k, acc_v), None)

    result, _ = lax.scan(
        sub_step, (zero_rows, zero_rows), (sub_queries, sub_grads, sub_log, sub_delta)
    )
    grad_k, grad_v = result
    grad_q_low = grad_q.reshape(1, shard_rows, width).astype(jnp.bfloat16)
    grad_k_low = grad_k.reshape(1, shard_rows, width).astype(jnp.bfloat16)
    grad_v_low = grad_v.reshape(1, shard_rows, width).astype(jnp.bfloat16)
    grad_query, grad_key, grad_value = (
        lax.all_to_all(grad_q_low, "head", split_axis=1, concat_axis=2, tiled=True),
        lax.all_to_all(grad_k_low, "head", split_axis=1, concat_axis=2, tiled=True),
        lax.all_to_all(grad_v_low, "head", split_axis=1, concat_axis=2, tiled=True),
    )
    return (grad_query, grad_key, grad_value)


def solution(mesh):
    sections, nh, nb = (mesh.shape[a] for a in ("section", "head", "blk"))

    def per_device(query_states, key_states, value_states, grad_next, valid_count):
        lay = Layout(query_states.shape[1], query_states.shape[2], nb, nh)
        powers = nb & (nb - 1) == 0 and nh & (nh - 1) == 0 and nb > 1
        args = (query_states, key_states, value_states, grad_next, valid_count)
        if powers and lay.heads % nb == 0 and lay.part % 16 == 0:
            return split_heads_program(lay, *args, sections)
        return gathered_program(*args)

    return jax.shard_map(
        per_device,
        mesh=mesh,
        in_specs=(
            P("section", "blk", "head"),
            P("section", "blk", "head"),
            P("section", "blk", "head"),
            P("section", ("blk", "head"), None),
            P("section"),
        ),
        out_specs=(
            P("section", ("blk", "head"), None),
            P("section", ("blk", "head"), None),
            P("section", ("blk", "head"), None),
        ),
        check_vma=False,
    )
```

```python
import functools
import math

import jax
import jax.numpy as jnp
from jax import lax
from jax.experimental import pallas as pl
from jax.experimental.pallas import tpu as pltpu
from jax.sharding import PartitionSpec as P

HD = 128
LOG2E = math.log2(math.e)
MASKED = -1e30
NT = (((1,), (1,)), ((), ()))
VMEM_LIMIT = 60 * 2**20
BUSY, BRIEF = 40_000_000_000, 1


def cols(index):
    return pl.ds(pl.multiple_of(index * HD, HD), HD)


def run_copies(pairs, sems):
    copies = [pltpu.make_async_copy(src, dst, sems.at[i]) for i, (src, dst) in enumerate(pairs)]
    for copy in copies:
        copy.start()
    for copy in copies:
        copy.wait()


def run_staged(pairs, stage, sems):
    loads, stores = [], []
    for i, (src, dst) in enumerate(pairs):
        buf = stage.at[i, pl.ds(0, src.shape[0]), :]
        loads.append(pltpu.make_async_copy(src, buf, sems.at[0, i]))
        stores.append(pltpu.make_async_copy(buf, dst, sems.at[1, i]))
    for load in loads:
        load.start()
    for load, store in zip(loads, stores):
        load.wait()
        store.start()
    for store in stores:
        store.wait()


class Chain:
    def __init__(self, resident):
        self.resident = resident
        self.token = jnp.zeros((8, HD), jnp.float32)

    def call(self, body, place, operands, out_shapes, aliases=None, **kwargs):
        any_space = pl.BlockSpec(memory_space=pl.ANY)
        in_hbm = pl.BlockSpec(memory_space=pltpu.HBM)
        spaces = [in_hbm if any(x is a for a in self.resident) else any_space for x in operands]
        n_in, n_out = len(operands), len(out_shapes)

        def whole(place_ref, *refs):
            body(place_ref, refs[1 : n_in + 1], refs[n_in + 2 : n_in + 2 + n_out], refs[n_in + 2 + n_out :])

        self.token, *outs = pl.pallas_call(
            whole,
            out_shape=(jax.ShapeDtypeStruct(self.token.shape, self.token.dtype), *out_shapes),
            in_specs=[pl.BlockSpec(memory_space=pltpu.SMEM), any_space, *spaces],
            out_specs=(any_space,) * (n_out + 1),
            input_output_aliases={i + 2: o + 1 for i, o in (aliases or {}).items()},
            **kwargs,
        )(place, self.token, *operands)
        return outs


def copy_kernel(chain, plan, count, rows, out_shapes, place, operands, name, aliases=None, weight=BUSY):
    def body(place_ref, ins, outs, scratch):
        run_staged(plan(place_ref, ins, outs), *scratch)

    moved = count * rows * HD * 2
    return chain.call(
        body,
        place,
        operands,
        out_shapes,
        aliases,
        scratch_shapes=[
            pltpu.VMEM((count, rows, HD), jnp.bfloat16),
            pltpu.SemaphoreType.DMA((2, count)),
        ],
        compiler_params=pltpu.CompilerParams(vmem_limit_bytes=VMEM_LIMIT),
        cost_estimate=pl.CostEstimate(flops=weight, bytes_accessed=1, transcendentals=0),
        name=name,
    )


class Layout:
    def __init__(self, rows, width, nb, nh):
        self.rows, self.nb, self.nh = rows, nb, nh
        self.heads = width // HD
        self.per = self.heads // nb
        self.nx = nb // 2
        self.part = rows // nh
        self.seq = rows * nb


def bf16(*shape):
    return jax.ShapeDtypeStruct(shape, jnp.bfloat16)


def attention_body(lay, bq, tk, run2, place, q_s, k_s, v_s, g_s, dq_s, dk_s, dv_s, e_s, d_s, m_s, kt_s, ak_s, av_s, dqt_s, qw_s, kw_s):
    seq, rows = lay.seq, lay.rows
    nq, nt = seq // bq, seq // tk
    c = HD**-0.5 * LOG2E
    limit, blk = place[0], place[1]
    live = [jnp.clip(limit - (blk ^ k) * rows, 0, rows) for k in range(lay.nb)]
    full = limit >= seq

    @pl.when(jnp.logical_not(full))
    def _():
        for k in range(lay.nb):
            span = slice(k * rows, (k + 1) * rows)
            row = lax.broadcasted_iota(jnp.int32, (rows, HD), 0)
            zeros = jnp.zeros((rows, HD), jnp.bfloat16)
            g_s[span, :] = jnp.where(row < live[k], g_s[span, :], zeros)
            first = lax.broadcasted_iota(jnp.int32, (rows, HD), 1) == 0
            qw_s[span, :HD] = q_s[span, :]
            qw_s[span, HD:] = jnp.where(first, 1.0, 0.0).astype(jnp.bfloat16)
            kw_s[span, :HD] = k_s[span, :]
            kw_s[span, HD:] = jnp.where(first & (row >= live[k]), MASKED, 0.0).astype(jnp.bfloat16)

    for t in range(nt):
        kt_s[t] = k_s[t * tk : (t + 1) * tk, :].T
    ak_s[...] = jnp.zeros_like(ak_s)
    av_s[...] = jnp.zeros_like(av_s)

    def run(masked):
        q_in, k_in = (qw_s, kw_s) if masked else (q_s, k_s)

        def step(i, carry):
            off = pl.multiple_of(i * bq, bq)
            qb = q_s[pl.ds(off, bq), :]
            qa = q_in[pl.ds(off, bq), :]
            gb = g_s[pl.ds(off, bq), :]
            top = jnp.full((1, bq), 2 * MASKED, jnp.float32)
            total = jnp.zeros((1, bq), jnp.float32)
            dot = total
            for t in range(nt):
                span = slice(t * tk, (t + 1) * tk)
                s = lax.dot_general(k_in[span, :], qa, NT, preferred_element_type=jnp.float32) * c
                new = jnp.maximum(top, jnp.max(s, axis=0, keepdims=True))
                e = jnp.exp2(s - new)
                d = lax.dot_general(v_s[span, :], gb, NT, preferred_element_type=jnp.float32)
                e_s[span, :] = e
                d_s[span, :] = d
                m_s[t] = new
                fade = jnp.exp2(top - new)
                total = total * fade + jnp.sum(e, axis=0, keepdims=True)
                dot = dot * fade + jnp.sum(e * d, axis=0, keepdims=True)
                top = new
            delta = dot / total
            lse = top + jnp.log2(total)
            dqt_s[...] = jnp.zeros_like(dqt_s)

            def tiles(j, carry):
                sum_q = jnp.zeros((HD, bq), jnp.float32)
                for u in range(run2):
                    t = j * run2 + u
                    span = pl.ds(pl.multiple_of(t * tk, tk), tk)
                    p = e_s[span, :] * jnp.exp2(m_s[t] - lse)
                    ds = (p * (d_s[span, :] - delta)).astype(jnp.bfloat16)
                    pb = p.astype(jnp.bfloat16)
                    av_s[span, :] += jnp.dot(pb, gb, preferred_element_type=jnp.float32)
                    ak_s[span, :] += jnp.dot(ds, qb, preferred_element_type=jnp.float32)
                    sum_q += jnp.dot(kt_s[t], ds, preferred_element_type=jnp.float32)
                dqt_s[...] += sum_q
                return carry

            lax.fori_loop(0, nt // run2, tiles, 0)
            dq_s[pl.ds(off, bq), :] = (dqt_s[...] * HD**-0.5).T.astype(jnp.bfloat16)
            return carry

        lax.fori_loop(0, nq, step, 0)

    pl.when(full)(lambda: run(False))
    pl.when(jnp.logical_not(full))(lambda: run(True))
    dk_s[...] = (ak_s[...] * HD**-0.5).astype(jnp.bfloat16)
    dv_s[...] = av_s[...].astype(jnp.bfloat16)


def attention(chain, lay, place, sources, operands, name):
    seq, part = lay.seq, lay.part
    bq, tk = math.gcd(1024, seq), math.gcd(256, lay.rows)
    run2 = math.gcd(4, seq // tk)
    def body(place_ref, ins, outs, scratch):
        bufs, results, work, sems = scratch[:4], scratch[4:7], scratch[7:-1], scratch[-1]
        pairs = [
            (src, buf.at[pl.ds(start, size), :])
            for buf, listing in zip(bufs, sources(place_ref, ins))
            for start, size, src in listing
        ]
        run_copies(pairs, sems)
        attention_body(lay, bq, tk, run2, place_ref, *bufs, *results, *work)
        run_copies(
            [
                (
                    results[t].at[pl.ds((k * lay.nh + h) * part, part), :],
                    outs[0].at[h * lay.nb + (place_ref[1] ^ k), t],
                )
                for h in range(lay.nh)
                for k in range(lay.nb)
                for t in range(3)
            ],
            sems,
        )

    flops = 2 * seq * seq * HD
    vec = lambda *s: pltpu.VMEM(s, jnp.bfloat16)
    acc = lambda *s: pltpu.VMEM(s, jnp.float32)
    n_sems = 4 * lay.nb * lay.nh
    return chain.call(
        body,
        place,
        operands,
        [bf16(lay.nh * lay.nb, 3, part, HD)],
        scratch_shapes=[vec(seq, HD)] * 7
        + [acc(seq, bq), acc(seq, bq), acc(seq // tk, 1, bq), vec(seq // tk, HD, tk)]
        + [acc(seq, HD), acc(seq, HD), acc(HD, bq), vec(seq, 2 * HD), vec(seq, 2 * HD)]
        + [pltpu.SemaphoreType.DMA((n_sems,))],
        compiler_params=pltpu.CompilerParams(vmem_limit_bytes=VMEM_LIMIT),
        cost_estimate=pl.CostEstimate(flops=400_000_000_000, bytes_accessed=1, transcendentals=0),
        name=name,
    )


def split_heads_program(lay, query_states, key_states, value_states, grad_next, valid_count, sections):
    nb, nh, nx, per, part, rows, heads = lay.nb, lay.nh, lay.nx, lay.per, lay.part, lay.rows, lay.heads
    blk, head = lax.axis_index("blk"), lax.axis_index("head")
    place = jnp.stack([valid_count[0], blk, head]).astype(jnp.int32)
    qkv = [query_states, key_states, value_states]
    chain = Chain([*qkv, grad_next])

    def grad_rows(at, refs, i, dest):
        return [(pl.multiple_of((at[2] ^ kh) * part, part), part, refs[kh].at[i, dest]) for kh in range(nh)]

    def send_grads(group):
        def plan(at, ins, outs):
            pairs = []
            for kh in range(nh):
                for i, c in enumerate(group):
                    for o in range(nb):
                        src = ins[0].at[0, :, cols((at[2] ^ kh) * heads + o * per + c)]
                        pairs.append((src, outs[kh].at[i, o]))
            return pairs

        shape = bf16(len(group), nb, part, HD)
        count = nh * len(group) * nb
        packed = copy_kernel(
            chain, plan, count, part, [shape] * nh, place, [grad_next], f"pack_grads_{group[0]}",
            weight=BRIEF if group[0] < 2 else BUSY,
        )
        moved = []
        for kh in range(nh):
            route = [
                (s * nh + h, (s - 1) % sections * nh + (h ^ kh))
                for s in range(sections)
                for h in range(nh)
            ]
            moved.append(lax.ppermute(packed[kh], ("section", "head"), route))
        return {c: (moved, i) for i, c in enumerate(group)}

    def blk_send(x, k):
        return lax.ppermute(x, "blk", [(i, i ^ k) for i in range(nb)])

    def send_far(c, kx, tensors, grads, name):
        refs, slot = grads if grads else ([], 0)
        extra = 1 if grads else 0

        def plan(at, ins, outs):
            pairs = []
            for j in range(2):
                dest = at[1] ^ (2 * kx + j)
                for t in range(len(tensors)):
                    pairs.append((ins[t].at[0, :, cols(dest * per + c)], outs[0].at[t, j]))
                if extra:
                    for start, size, src in grad_rows(at, ins[len(tensors) :], slot, dest):
                        pairs.append((src, outs[0].at[len(tensors), j, pl.ds(start, size), :]))
            return pairs

        n = 2 * (len(tensors) + extra * nh)
        shape = bf16(len(tensors) + extra, 2, rows, HD)
        weight = BRIEF if c == 0 or (c == 1 and tensors) else BUSY
        packed = copy_kernel(chain, plan, n, rows, [shape], place, [*tensors, *refs], name, weight=weight)
        return blk_send(packed[0], 2 * kx)

    def send_near(c, grads, far):
        refs, slot = grads

        def plan(at, ins, outs):
            pairs = []
            dest = at[1] ^ 1
            for t in range(3):
                pairs.append((ins[t].at[0, :, cols(dest * per + c)], outs[0].at[t, 0]))
            for start, size, src in grad_rows(at, ins[3 : 3 + nh], slot, dest):
                pairs.append((src, outs[0].at[3, 0, pl.ds(start, size), :]))
            rest = iter(ins[3 + nh :])
            for kx in range(1, nx):
                for begin, count, _ in far[kx]:
                    ref = next(rest)
                    for t in range(count):
                        pairs.append((ref.at[t, 1], outs[0].at[begin + t, kx]))
            return pairs

        arrays = [a for kx in range(1, nx) for _, _, a in far[kx]]
        n = 3 + nh + 4 * (nx - 1)
        packed = copy_kernel(
            chain, plan, n, rows, [bf16(4, nx, rows, HD)], place, [*qkv, *refs, *arrays], f"pack_near_{c}"
        )
        return blk_send(packed[0], 1)

    def attend(c, grads, far, near):
        refs, slot = grads

        def sources(at, ins):
            near_ref = ins[3 + nh]
            far_refs = iter(ins[4 + nh :])
            listing = [[], [], [], []]
            for t in range(3):
                listing[t].append((0, rows, ins[t].at[0, :, cols(at[1] * per + c)]))
            listing[3].extend(grad_rows(at, ins[3 : 3 + nh], slot, at[1]))
            for kx in range(nx):
                for t in range(4):
                    listing[t].append(((2 * kx + 1) * rows, rows, near_ref.at[t, kx]))
            for kx in range(1, nx):
                for begin, count, _ in far[kx]:
                    ref = next(far_refs)
                    for t in range(count):
                        listing[begin + t].append((2 * kx * rows, rows, ref.at[t, 0]))
            return listing

        arrays = [a for kx in range(1, nx) for _, _, a in far[kx]]
        sent = attention(chain, lay, place, sources, [*qkv, *refs, near, *arrays], f"attention_{c}")
        return lax.all_to_all(sent[0], ("head", "blk"), split_axis=0, concat_axis=0, tiled=True)

    def place_outputs(c, got, outs):
        def plan(at, ins, out_refs):
            return [
                (ins[0].at[h * nb + o, t], out_refs[t].at[0, :, cols(h * heads + o * per + c)])
                for h in range(nh)
                for o in range(nb)
                for t in range(3)
            ]

        shape = bf16(1, part, nh * heads * HD)
        aliases = {1 + t: t for t in range(3)} if outs else None
        operands = [got, *(outs or [])]
        return copy_kernel(
            chain, plan, 3 * nh * nb, part, [shape] * 3, place, operands, f"unpack_{c}", aliases
        )

    fars = range(1, nx)
    far, near, grads, got, outs = {}, {}, {}, {}, None

    def far_tensors(c, tensors, cotangent, first):
        for kx in fars:
            name = f"pack_far_{c}_{kx}_{first}"
            count = len(tensors) + (1 if cotangent else 0)
            x = send_far(c, kx, tensors, grads[c] if cotangent else None, name)
            far.setdefault(c, {}).setdefault(kx, []).append((first, count, x))

    far_tensors(0, qkv, False, 0)
    grads.update(send_grads([0]))
    if per > 1:
        grads.update(send_grads([1]))
        far_tensors(1, qkv, False, 0)
    far_tensors(0, [], True, 3)
    near[0] = send_near(0, grads[0], far[0])
    if per > 1:
        far_tensors(1, [], True, 3)
    if per > 2:
        grads.update(send_grads(list(range(2, per))))
        far_tensors(2, qkv, False, 0)
    for c in range(per):
        got[c] = attend(c, grads[c], far[c], near[c])
        if c + 1 < per:
            near[c + 1] = send_near(c + 1, grads[c + 1], far[c + 1])
        if c + 2 < per and c == 0:
            far_tensors(2, [], True, 3)
        if c + 3 < per:
            far_tensors(c + 3, qkv, True, 0)
        if c > 0:
            outs = place_outputs(c - 1, got[c - 1], outs)
    outs = place_outputs(per - 1, got[per - 1], outs)
    return tuple(outs)


def shifted(x, axis, by):
    peers = lax.axis_size(axis)
    return lax.ppermute(x, axis, [(i, (i + by) % peers) for i in range(peers)])


def masked_scores(query_block, key_block, key_positions, limit):
    scores = jnp.einsum(
        "qhd,khd->hqk", query_block, key_block, preferred_element_type=jnp.float32
    ) * HD ** (-0.5)
    return jnp.where(key_positions[None, None, :] < limit, scores, -jnp.inf)


def gathered_program(query_states, key_states, value_states, grad_next, valid_count):
    scale = HD ** (-0.5)
    blk_index = lax.axis_index("blk")
    incoming = shifted(grad_next, "section", -1)
    grads = lax.all_to_all(incoming, "head", split_axis=2, concat_axis=1, tiled=True)
    shard_rows = query_states.shape[1]
    width = query_states.shape[2]
    local_heads = width // HD
    limit = valid_count[0]
    own_positions = blk_index * shard_rows + jnp.arange(shard_rows, dtype=jnp.int32)
    grads = jnp.where((own_positions < limit)[None, :, None], grads, jnp.zeros_like(grads))
    query_heads = query_states[0].reshape(shard_rows, local_heads, HD)
    grad_heads = grads[0].reshape(shard_rows, local_heads, HD)
    gathered_keys, gathered_values = (
        lax.all_gather(key_states, "blk", axis=1, tiled=True),
        lax.all_gather(value_states, "blk", axis=1, tiled=True),
    )
    key_count = gathered_keys.shape[1]
    block_rows = math.gcd(512, key_count)
    block_count = key_count // block_rows
    key_blocks = gathered_keys[0].reshape(block_count, block_rows, local_heads, HD)
    value_blocks = gathered_values[0].reshape(block_count, block_rows, local_heads, HD)
    position_blocks = jnp.arange(key_count, dtype=jnp.int32).reshape(block_count, block_rows)

    def forward_step(carry, block):
        run_max, run_sum, run_dot = carry
        key_block, value_block, key_pos = block
        scores = masked_scores(query_heads, key_block, key_pos, limit)
        grad_probs = jnp.einsum(
            "qhd,khd->hqk", grad_heads, value_block, preferred_element_type=jnp.float32
        )
        new_max = jnp.maximum(run_max, jnp.max(scores, axis=2))
        factor = jnp.exp(run_max - new_max)
        weights = jnp.exp(scores - new_max[:, :, None])
        run_sum = run_sum * factor + jnp.sum(weights, axis=2)
        run_dot = run_dot * factor + jnp.sum(weights * grad_probs, axis=2)
        return ((new_max, run_sum, run_dot), None)

    start_max = jnp.full((local_heads, shard_rows), -jnp.inf, jnp.float32)
    start_zero = jnp.zeros((local_heads, shard_rows), jnp.float32)
    (run_max, run_sum, run_dot), _ = lax.scan(
        forward_step,
        (start_max, start_zero, start_zero),
        (key_blocks, value_blocks, position_blocks),
    )
    log_total = run_max + jnp.log(run_sum)
    delta = run_dot / run_sum

    def block_terms(
        query_block, grad_block, key_block, value_block, key_pos, block_log, block_delta
    ):
        scores = masked_scores(query_block, key_block, key_pos, limit)
        probs = jnp.exp(scores - block_log[:, :, None])
        grad_probs = jnp.einsum(
            "qhd,khd->hqk", grad_block, value_block, preferred_element_type=jnp.float32
        )
        grad_scores = (probs * (grad_probs - block_delta[:, :, None])).astype(jnp.bfloat16)
        return (probs.astype(jnp.bfloat16), grad_scores)

    zero_rows = jnp.zeros((shard_rows, local_heads, HD), jnp.float32)

    def query_step(grad_q, block):
        key_block, value_block, key_pos = block
        prob_low, grad_scores = block_terms(
            query_heads, grad_heads, key_block, value_block, key_pos, log_total, delta
        )
        grad_q = (
            grad_q
            + jnp.einsum("hqk,khd->qhd", grad_scores, key_block, preferred_element_type=jnp.float32)
            * scale
        )
        return (grad_q, None)

    grad_q, _ = lax.scan(query_step, zero_rows, (key_blocks, value_blocks, position_blocks))
    all_log, all_delta = (
        lax.all_gather(log_total.T[None], "blk", axis=1, tiled=True),
        lax.all_gather(delta.T[None], "blk", axis=1, tiled=True),
    )
    key_heads = key_states[0].reshape(shard_rows, local_heads, HD)
    value_heads = value_states[0].reshape(shard_rows, local_heads, HD)
    piece_queries = lax.all_gather(query_states, "blk", axis=1, tiled=True)
    piece_grads = lax.all_gather(grads, "blk", axis=1, tiled=True)
    piece_rows = piece_queries.shape[1]
    sub_rows = math.gcd(shard_rows, piece_rows)
    sub_count = piece_rows // sub_rows
    piece_log = all_log[0]
    piece_delta = all_delta[0]
    sub_queries = piece_queries[0].reshape(sub_count, sub_rows, local_heads, HD)
    sub_grads = piece_grads[0].reshape(sub_count, sub_rows, local_heads, HD)
    sub_log = piece_log.reshape(sub_count, sub_rows, local_heads)
    sub_delta = piece_delta.reshape(sub_count, sub_rows, local_heads)

    def sub_step(accum, sub):
        acc_k, acc_v = accum
        query_block, grad_block, block_log, block_delta = sub
        prob_low, grad_scores = block_terms(
            query_block,
            grad_block,
            key_heads,
            value_heads,
            own_positions,
            block_log.T,
            block_delta.T,
        )
        acc_v = acc_v + jnp.einsum(
            "hqk,qhd->khd", prob_low, grad_block, preferred_element_type=jnp.float32
        )
        acc_k = (
            acc_k
            + jnp.einsum(
                "hqk,qhd->khd", grad_scores, query_block, preferred_element_type=jnp.float32
            )
            * scale
        )
        return ((acc_k, acc_v), None)

    result, _ = lax.scan(
        sub_step, (zero_rows, zero_rows), (sub_queries, sub_grads, sub_log, sub_delta)
    )
    grad_k, grad_v = result
    grad_q_low = grad_q.reshape(1, shard_rows, width).astype(jnp.bfloat16)
    grad_k_low = grad_k.reshape(1, shard_rows, width).astype(jnp.bfloat16)
    grad_v_low = grad_v.reshape(1, shard_rows, width).astype(jnp.bfloat16)
    grad_query, grad_key, grad_value = (
        lax.all_to_all(grad_q_low, "head", split_axis=1, concat_axis=2, tiled=True),
        lax.all_to_all(grad_k_low, "head", split_axis=1, concat_axis=2, tiled=True),
        lax.all_to_all(grad_v_low, "head", split_axis=1, concat_axis=2, tiled=True),
    )
    return (grad_query, grad_key, grad_value)


def solution(mesh):
    sections, nh, nb = (mesh.shape[a] for a in ("section", "head", "blk"))

    def per_device(query_states, key_states, value_states, grad_next, valid_count):
        lay = Layout(query_states.shape[1], query_states.shape[2], nb, nh)
        powers = nb & (nb - 1) == 0 and nh & (nh - 1) == 0 and nb > 1
        args = (query_states, key_states, value_states, grad_next, valid_count)
        if powers and lay.heads % nb == 0 and lay.part % 16 == 0:
            return split_heads_program(lay, *args, sections)
        return gathered_program(*args)

    return jax.shard_map(
        per_device,
        mesh=mesh,
        in_specs=(
            P("section", "blk", "head"),
            P("section", "blk", "head"),
            P("section", "blk", "head"),
            P("section", ("blk", "head"), None),
            P("section"),
        ),
        out_specs=(
            P("section", ("blk", "head"), None),
            P("section", ("blk", "head"), None),
            P("section", ("blk", "head"), None),
        ),
        check_vma=False,
    )
```

```python
import functools
import math

import jax
import jax.numpy as jnp
from jax import lax
from jax.experimental import pallas as pl
from jax.experimental.pallas import tpu as pltpu
from jax.sharding import PartitionSpec as P

HD = 128
LOG2E = math.log2(math.e)
MASKED = -1e30
NT = (((1,), (1,)), ((), ()))
VMEM_LIMIT = 60 * 2**20
BUSY, BRIEF = 40_000_000_000, 1


def cols(index):
    return pl.ds(pl.multiple_of(index * HD, HD), HD)


def run_copies(pairs, sems):
    copies = [pltpu.make_async_copy(src, dst, sems.at[i]) for i, (src, dst) in enumerate(pairs)]
    for copy in copies:
        copy.start()
    for copy in copies:
        copy.wait()


def run_staged(pairs, stage, sems):
    loads, stores = [], []
    for i, (src, dst) in enumerate(pairs):
        buf = stage.at[i, pl.ds(0, src.shape[0]), :]
        loads.append(pltpu.make_async_copy(src, buf, sems.at[0, i]))
        stores.append(pltpu.make_async_copy(buf, dst, sems.at[1, i]))
    for load in loads:
        load.start()
    for load, store in zip(loads, stores):
        load.wait()
        store.start()
    for store in stores:
        store.wait()


class Chain:
    def __init__(self, resident):
        self.resident = resident
        self.token = jnp.zeros((8, HD), jnp.float32)

    def call(self, body, place, operands, out_shapes, aliases=None, **kwargs):
        any_space = pl.BlockSpec(memory_space=pl.ANY)
        in_hbm = pl.BlockSpec(memory_space=pltpu.HBM)
        spaces = [in_hbm if any(x is a for a in self.resident) else any_space for x in operands]
        n_in, n_out = len(operands), len(out_shapes)

        def whole(place_ref, *refs):
            body(place_ref, refs[1 : n_in + 1], refs[n_in + 2 : n_in + 2 + n_out], refs[n_in + 2 + n_out :])

        self.token, *outs = pl.pallas_call(
            whole,
            out_shape=(jax.ShapeDtypeStruct(self.token.shape, self.token.dtype), *out_shapes),
            in_specs=[pl.BlockSpec(memory_space=pltpu.SMEM), any_space, *spaces],
            out_specs=(any_space,) * (n_out + 1),
            input_output_aliases={i + 2: o + 1 for i, o in (aliases or {}).items()},
            **kwargs,
        )(place, self.token, *operands)
        return outs


def copy_kernel(chain, plan, count, rows, out_shapes, place, operands, name, aliases=None, weight=BUSY):
    def body(place_ref, ins, outs, scratch):
        run_staged(plan(place_ref, ins, outs), *scratch)

    moved = count * rows * HD * 2
    return chain.call(
        body,
        place,
        operands,
        out_shapes,
        aliases,
        scratch_shapes=[
            pltpu.VMEM((count, rows, HD), jnp.bfloat16),
            pltpu.SemaphoreType.DMA((2, count)),
        ],
        compiler_params=pltpu.CompilerParams(vmem_limit_bytes=VMEM_LIMIT),
        cost_estimate=pl.CostEstimate(flops=weight, bytes_accessed=1, transcendentals=0),
        name=name,
    )


class Layout:
    def __init__(self, rows, width, nb, nh):
        self.rows, self.nb, self.nh = rows, nb, nh
        self.heads = width // HD
        self.per = self.heads // nb
        self.nx = nb // 2
        self.part = rows // nh
        self.seq = rows * nb


def bf16(*shape):
    return jax.ShapeDtypeStruct(shape, jnp.bfloat16)


def attention_body(lay, bq, tk, run2, place, q_s, k_s, v_s, g_s, dq_s, dk_s, dv_s, e_s, d_s, m_s, kt_s, ak_s, av_s, dqt_s, qw_s, kw_s):
    seq, rows = lay.seq, lay.rows
    nq, nt = seq // bq, seq // tk
    c = HD**-0.5 * LOG2E
    limit, blk = place[0], place[1]
    live = [jnp.clip(limit - (blk ^ k) * rows, 0, rows) for k in range(lay.nb)]
    full = limit >= seq

    @pl.when(jnp.logical_not(full))
    def _():
        for k in range(lay.nb):
            span = slice(k * rows, (k + 1) * rows)
            row = lax.broadcasted_iota(jnp.int32, (rows, HD), 0)
            zeros = jnp.zeros((rows, HD), jnp.bfloat16)
            g_s[span, :] = jnp.where(row < live[k], g_s[span, :], zeros)
            first = lax.broadcasted_iota(jnp.int32, (rows, HD), 1) == 0
            qw_s[span, :HD] = q_s[span, :]
            qw_s[span, HD:] = jnp.where(first, 1.0, 0.0).astype(jnp.bfloat16)
            kw_s[span, :HD] = k_s[span, :]
            kw_s[span, HD:] = jnp.where(first & (row >= live[k]), MASKED, 0.0).astype(jnp.bfloat16)

    for t in range(nt):
        kt_s[t] = k_s[t * tk : (t + 1) * tk, :].T
    ak_s[...] = jnp.zeros_like(ak_s)
    av_s[...] = jnp.zeros_like(av_s)

    def run(masked):
        q_in, k_in = (qw_s, kw_s) if masked else (q_s, k_s)

        def step(i, carry):
            off = pl.multiple_of(i * bq, bq)
            qb = q_s[pl.ds(off, bq), :]
            qa = q_in[pl.ds(off, bq), :]
            gb = g_s[pl.ds(off, bq), :]
            top = jnp.full((1, bq), 2 * MASKED, jnp.float32)
            total = jnp.zeros((1, bq), jnp.float32)
            dot = total
            for t in range(nt):
                span = slice(t * tk, (t + 1) * tk)
                s = lax.dot_general(k_in[span, :], qa, NT, preferred_element_type=jnp.float32) * c
                new = jnp.maximum(top, jnp.max(s, axis=0, keepdims=True))
                e = jnp.exp2(s - new)
                d = lax.dot_general(v_s[span, :], gb, NT, preferred_element_type=jnp.float32)
                e_s[span, :] = e
                d_s[span, :] = d
                m_s[t] = new
                fade = jnp.exp2(top - new)
                total = total * fade + jnp.sum(e, axis=0, keepdims=True)
                dot = dot * fade + jnp.sum(e * d, axis=0, keepdims=True)
                top = new
            delta = dot / total
            lse = top + jnp.log2(total)
            dqt_s[...] = jnp.zeros_like(dqt_s)

            def tiles(j, carry):
                sum_q = jnp.zeros((HD, bq), jnp.float32)
                for u in range(run2):
                    t = j * run2 + u
                    span = pl.ds(pl.multiple_of(t * tk, tk), tk)
                    p = e_s[span, :] * jnp.exp2(m_s[t] - lse)
                    ds = (p * (d_s[span, :] - delta)).astype(jnp.bfloat16)
                    pb = p.astype(jnp.bfloat16)
                    av_s[span, :] += jnp.dot(pb, gb, preferred_element_type=jnp.float32)
                    ak_s[span, :] += jnp.dot(ds, qb, preferred_element_type=jnp.float32)
                    sum_q += jnp.dot(kt_s[t], ds, preferred_element_type=jnp.float32)
                dqt_s[...] += sum_q
                return carry

            lax.fori_loop(0, nt // run2, tiles, 0)
            dq_s[pl.ds(off, bq), :] = (dqt_s[...] * HD**-0.5).T.astype(jnp.bfloat16)
            return carry

        lax.fori_loop(0, nq, step, 0)

    pl.when(full)(lambda: run(False))
    pl.when(jnp.logical_not(full))(lambda: run(True))
    dk_s[...] = (ak_s[...] * HD**-0.5).astype(jnp.bfloat16)
    dv_s[...] = av_s[...].astype(jnp.bfloat16)


def attention(chain, lay, place, sources, operands, name):
    seq, part = lay.seq, lay.part
    bq, tk = math.gcd(1024, seq), math.gcd(256, lay.rows)
    run2 = math.gcd(4, seq // tk)
    def body(place_ref, ins, outs, scratch):
        bufs, results, work, sems = scratch[:4], scratch[4:7], scratch[7:-1], scratch[-1]
        pairs = [
            (src, buf.at[pl.ds(start, size), :])
            for buf, listing in zip(bufs, sources(place_ref, ins))
            for start, size, src in listing
        ]
        run_copies(pairs, sems)
        attention_body(lay, bq, tk, run2, place_ref, *bufs, *results, *work)
        run_copies(
            [
                (
                    results[t].at[pl.ds((k * lay.nh + h) * part, part), :],
                    outs[0].at[h * lay.nb + (place_ref[1] ^ k), t],
                )
                for h in range(lay.nh)
                for k in range(lay.nb)
                for t in range(3)
            ],
            sems,
        )

    flops = 2 * seq * seq * HD
    vec = lambda *s: pltpu.VMEM(s, jnp.bfloat16)
    acc = lambda *s: pltpu.VMEM(s, jnp.float32)
    n_sems = 4 * lay.nb * lay.nh
    return chain.call(
        body,
        place,
        operands,
        [bf16(lay.nh * lay.nb, 3, part, HD)],
        scratch_shapes=[vec(seq, HD)] * 7
        + [acc(seq, bq), acc(seq, bq), acc(seq // tk, 1, bq), vec(seq // tk, HD, tk)]
        + [acc(seq, HD), acc(seq, HD), acc(HD, bq), vec(seq, 2 * HD), vec(seq, 2 * HD)]
        + [pltpu.SemaphoreType.DMA((n_sems,))],
        compiler_params=pltpu.CompilerParams(vmem_limit_bytes=VMEM_LIMIT),
        cost_estimate=pl.CostEstimate(flops=400_000_000_000, bytes_accessed=1, transcendentals=0),
        name=name,
    )


def split_heads_program(lay, query_states, key_states, value_states, grad_next, valid_count, sections):
    nb, nh, nx, per, part, rows, heads = lay.nb, lay.nh, lay.nx, lay.per, lay.part, lay.rows, lay.heads
    blk, head = lax.axis_index("blk"), lax.axis_index("head")
    place = jnp.stack([valid_count[0], blk, head]).astype(jnp.int32)
    qkv = [query_states, key_states, value_states]
    chain = Chain([*qkv, grad_next])

    def grad_rows(at, refs, i, dest):
        return [(pl.multiple_of((at[2] ^ kh) * part, part), part, refs[kh].at[i, dest]) for kh in range(nh)]

    def send_grads(group):
        def plan(at, ins, outs):
            pairs = []
            for kh in range(nh):
                for i, c in enumerate(group):
                    for o in range(nb):
                        src = ins[0].at[0, :, cols((at[2] ^ kh) * heads + o * per + c)]
                        pairs.append((src, outs[kh].at[i, o]))
            return pairs

        shape = bf16(len(group), nb, part, HD)
        count = nh * len(group) * nb
        packed = copy_kernel(
            chain, plan, count, part, [shape] * nh, place, [grad_next], f"pack_grads_{group[0]}",
            weight=BRIEF,
        )
        moved = []
        for kh in range(nh):
            route = [
                (s * nh + h, (s - 1) % sections * nh + (h ^ kh))
                for s in range(sections)
                for h in range(nh)
            ]
            moved.append(lax.ppermute(packed[kh], ("section", "head"), route))
        return {c: (moved, i) for i, c in enumerate(group)}

    def blk_send(x, k):
        return lax.ppermute(x, "blk", [(i, i ^ k) for i in range(nb)])

    def send_far(c, kx, tensors, grads, name):
        refs, slot = grads if grads else ([], 0)
        extra = 1 if grads else 0

        def plan(at, ins, outs):
            pairs = []
            for j in range(2):
                dest = at[1] ^ (2 * kx + j)
                for t in range(len(tensors)):
                    pairs.append((ins[t].at[0, :, cols(dest * per + c)], outs[0].at[t, j]))
                if extra:
                    for start, size, src in grad_rows(at, ins[len(tensors) :], slot, dest):
                        pairs.append((src, outs[0].at[len(tensors), j, pl.ds(start, size), :]))
            return pairs

        n = 2 * (len(tensors) + extra * nh)
        shape = bf16(len(tensors) + extra, 2, rows, HD)
        weight = BRIEF if c == 0 or (c == 1 and tensors) else BUSY
        packed = copy_kernel(chain, plan, n, rows, [shape], place, [*tensors, *refs], name, weight=weight)
        return blk_send(packed[0], 2 * kx)

    def send_near(c, grads, far):
        refs, slot = grads

        def plan(at, ins, outs):
            pairs = []
            dest = at[1] ^ 1
            for t in range(3):
                pairs.append((ins[t].at[0, :, cols(dest * per + c)], outs[0].at[t, 0]))
            for start, size, src in grad_rows(at, ins[3 : 3 + nh], slot, dest):
                pairs.append((src, outs[0].at[3, 0, pl.ds(start, size), :]))
            rest = iter(ins[3 + nh :])
            for kx in range(1, nx):
                for begin, count, _ in far[kx]:
                    ref = next(rest)
                    for t in range(count):
                        pairs.append((ref.at[t, 1], outs[0].at[begin + t, kx]))
            return pairs

        arrays = [a for kx in range(1, nx) for _, _, a in far[kx]]
        n = 3 + nh + 4 * (nx - 1)
        packed = copy_kernel(
            chain, plan, n, rows, [bf16(4, nx, rows, HD)], place, [*qkv, *refs, *arrays], f"pack_near_{c}"
        )
        return blk_send(packed[0], 1)

    def attend(c, grads, far, near):
        refs, slot = grads

        def sources(at, ins):
            near_ref = ins[3 + nh]
            far_refs = iter(ins[4 + nh :])
            listing = [[], [], [], []]
            for t in range(3):
                listing[t].append((0, rows, ins[t].at[0, :, cols(at[1] * per + c)]))
            listing[3].extend(grad_rows(at, ins[3 : 3 + nh], slot, at[1]))
            for kx in range(nx):
                for t in range(4):
                    listing[t].append(((2 * kx + 1) * rows, rows, near_ref.at[t, kx]))
            for kx in range(1, nx):
                for begin, count, _ in far[kx]:
                    ref = next(far_refs)
                    for t in range(count):
                        listing[begin + t].append((2 * kx * rows, rows, ref.at[t, 0]))
            return listing

        arrays = [a for kx in range(1, nx) for _, _, a in far[kx]]
        sent = attention(chain, lay, place, sources, [*qkv, *refs, near, *arrays], f"attention_{c}")
        return lax.all_to_all(sent[0], ("head", "blk"), split_axis=0, concat_axis=0, tiled=True)

    def place_outputs(c, got, outs):
        def plan(at, ins, out_refs):
            return [
                (ins[0].at[h * nb + o, t], out_refs[t].at[0, :, cols(h * heads + o * per + c)])
                for h in range(nh)
                for o in range(nb)
                for t in range(3)
            ]

        shape = bf16(1, part, nh * heads * HD)
        aliases = {1 + t: t for t in range(3)} if outs else None
        operands = [got, *(outs or [])]
        return copy_kernel(
            chain, plan, 3 * nh * nb, part, [shape] * 3, place, operands, f"unpack_{c}", aliases
        )

    fars = range(1, nx)
    far, near, grads, got, outs = {}, {}, {}, {}, None

    def far_tensors(c, tensors, cotangent, first):
        for kx in fars:
            name = f"pack_far_{c}_{kx}_{first}"
            count = len(tensors) + (1 if cotangent else 0)
            x = send_far(c, kx, tensors, grads[c] if cotangent else None, name)
            far.setdefault(c, {}).setdefault(kx, []).append((first, count, x))

    far_tensors(0, qkv, False, 0)
    grads.update(send_grads([0]))
    if per > 1:
        grads.update(send_grads([1]))
        if per > 2:
            grads.update(send_grads(list(range(2, per))))
        far_tensors(1, qkv, False, 0)
    far_tensors(0, [], True, 3)
    near[0] = send_near(0, grads[0], far[0])
    if per > 1:
        far_tensors(1, [], True, 3)
    if per > 2:
        far_tensors(2, qkv, False, 0)
    for c in range(per):
        got[c] = attend(c, grads[c], far[c], near[c])
        if c + 1 < per:
            near[c + 1] = send_near(c + 1, grads[c + 1], far[c + 1])
        if c + 2 < per and c == 0:
            far_tensors(2, [], True, 3)
        if c + 3 < per:
            far_tensors(c + 3, qkv, True, 0)
        if c > 0:
            outs = place_outputs(c - 1, got[c - 1], outs)
    outs = place_outputs(per - 1, got[per - 1], outs)
    return tuple(outs)


def shifted(x, axis, by):
    peers = lax.axis_size(axis)
    return lax.ppermute(x, axis, [(i, (i + by) % peers) for i in range(peers)])


def masked_scores(query_block, key_block, key_positions, limit):
    scores = jnp.einsum(
        "qhd,khd->hqk", query_block, key_block, preferred_element_type=jnp.float32
    ) * HD ** (-0.5)
    return jnp.where(key_positions[None, None, :] < limit, scores, -jnp.inf)


def gathered_program(query_states, key_states, value_states, grad_next, valid_count):
    scale = HD ** (-0.5)
    blk_index = lax.axis_index("blk")
    incoming = shifted(grad_next, "section", -1)
    grads = lax.all_to_all(incoming, "head", split_axis=2, concat_axis=1, tiled=True)
    shard_rows = query_states.shape[1]
    width = query_states.shape[2]
    local_heads = width // HD
    limit = valid_count[0]
    own_positions = blk_index * shard_rows + jnp.arange(shard_rows, dtype=jnp.int32)
    grads = jnp.where((own_positions < limit)[None, :, None], grads, jnp.zeros_like(grads))
    query_heads = query_states[0].reshape(shard_rows, local_heads, HD)
    grad_heads = grads[0].reshape(shard_rows, local_heads, HD)
    gathered_keys, gathered_values = (
        lax.all_gather(key_states, "blk", axis=1, tiled=True),
        lax.all_gather(value_states, "blk", axis=1, tiled=True),
    )
    key_count = gathered_keys.shape[1]
    block_rows = math.gcd(512, key_count)
    block_count = key_count // block_rows
    key_blocks = gathered_keys[0].reshape(block_count, block_rows, local_heads, HD)
    value_blocks = gathered_values[0].reshape(block_count, block_rows, local_heads, HD)
    position_blocks = jnp.arange(key_count, dtype=jnp.int32).reshape(block_count, block_rows)

    def forward_step(carry, block):
        run_max, run_sum, run_dot = carry
        key_block, value_block, key_pos = block
        scores = masked_scores(query_heads, key_block, key_pos, limit)
        grad_probs = jnp.einsum(
            "qhd,khd->hqk", grad_heads, value_block, preferred_element_type=jnp.float32
        )
        new_max = jnp.maximum(run_max, jnp.max(scores, axis=2))
        factor = jnp.exp(run_max - new_max)
        weights = jnp.exp(scores - new_max[:, :, None])
        run_sum = run_sum * factor + jnp.sum(weights, axis=2)
        run_dot = run_dot * factor + jnp.sum(weights * grad_probs, axis=2)
        return ((new_max, run_sum, run_dot), None)

    start_max = jnp.full((local_heads, shard_rows), -jnp.inf, jnp.float32)
    start_zero = jnp.zeros((local_heads, shard_rows), jnp.float32)
    (run_max, run_sum, run_dot), _ = lax.scan(
        forward_step,
        (start_max, start_zero, start_zero),
        (key_blocks, value_blocks, position_blocks),
    )
    log_total = run_max + jnp.log(run_sum)
    delta = run_dot / run_sum

    def block_terms(
        query_block, grad_block, key_block, value_block, key_pos, block_log, block_delta
    ):
        scores = masked_scores(query_block, key_block, key_pos, limit)
        probs = jnp.exp(scores - block_log[:, :, None])
        grad_probs = jnp.einsum(
            "qhd,khd->hqk", grad_block, value_block, preferred_element_type=jnp.float32
        )
        grad_scores = (probs * (grad_probs - block_delta[:, :, None])).astype(jnp.bfloat16)
        return (probs.astype(jnp.bfloat16), grad_scores)

    zero_rows = jnp.zeros((shard_rows, local_heads, HD), jnp.float32)

    def query_step(grad_q, block):
        key_block, value_block, key_pos = block
        prob_low, grad_scores = block_terms(
            query_heads, grad_heads, key_block, value_block, key_pos, log_total, delta
        )
        grad_q = (
            grad_q
            + jnp.einsum("hqk,khd->qhd", grad_scores, key_block, preferred_element_type=jnp.float32)
            * scale
        )
        return (grad_q, None)

    grad_q, _ = lax.scan(query_step, zero_rows, (key_blocks, value_blocks, position_blocks))
    all_log, all_delta = (
        lax.all_gather(log_total.T[None], "blk", axis=1, tiled=True),
        lax.all_gather(delta.T[None], "blk", axis=1, tiled=True),
    )
    key_heads = key_states[0].reshape(shard_rows, local_heads, HD)
    value_heads = value_states[0].reshape(shard_rows, local_heads, HD)
    piece_queries = lax.all_gather(query_states, "blk", axis=1, tiled=True)
    piece_grads = lax.all_gather(grads, "blk", axis=1, tiled=True)
    piece_rows = piece_queries.shape[1]
    sub_rows = math.gcd(shard_rows, piece_rows)
    sub_count = piece_rows // sub_rows
    piece_log = all_log[0]
    piece_delta = all_delta[0]
    sub_queries = piece_queries[0].reshape(sub_count, sub_rows, local_heads, HD)
    sub_grads = piece_grads[0].reshape(sub_count, sub_rows, local_heads, HD)
    sub_log = piece_log.reshape(sub_count, sub_rows, local_heads)
    sub_delta = piece_delta.reshape(sub_count, sub_rows, local_heads)

    def sub_step(accum, sub):
        acc_k, acc_v = accum
        query_block, grad_block, block_log, block_delta = sub
        prob_low, grad_scores = block_terms(
            query_block,
            grad_block,
            key_heads,
            value_heads,
            own_positions,
            block_log.T,
            block_delta.T,
        )
        acc_v = acc_v + jnp.einsum(
            "hqk,qhd->khd", prob_low, grad_block, preferred_element_type=jnp.float32
        )
        acc_k = (
            acc_k
            + jnp.einsum(
                "hqk,qhd->khd", grad_scores, query_block, preferred_element_type=jnp.float32
            )
            * scale
        )
        return ((acc_k, acc_v), None)

    result, _ = lax.scan(
        sub_step, (zero_rows, zero_rows), (sub_queries, sub_grads, sub_log, sub_delta)
    )
    grad_k, grad_v = result
    grad_q_low = grad_q.reshape(1, shard_rows, width).astype(jnp.bfloat16)
    grad_k_low = grad_k.reshape(1, shard_rows, width).astype(jnp.bfloat16)
    grad_v_low = grad_v.reshape(1, shard_rows, width).astype(jnp.bfloat16)
    grad_query, grad_key, grad_value = (
        lax.all_to_all(grad_q_low, "head", split_axis=1, concat_axis=2, tiled=True),
        lax.all_to_all(grad_k_low, "head", split_axis=1, concat_axis=2, tiled=True),
        lax.all_to_all(grad_v_low, "head", split_axis=1, concat_axis=2, tiled=True),
    )
    return (grad_query, grad_key, grad_value)


def solution(mesh):
    sections, nh, nb = (mesh.shape[a] for a in ("section", "head", "blk"))

    def per_device(query_states, key_states, value_states, grad_next, valid_count):
        lay = Layout(query_states.shape[1], query_states.shape[2], nb, nh)
        powers = nb & (nb - 1) == 0 and nh & (nh - 1) == 0 and nb > 1
        args = (query_states, key_states, value_states, grad_next, valid_count)
        if powers and lay.heads % nb == 0 and lay.part % 16 == 0:
            return split_heads_program(lay, *args, sections)
        return gathered_program(*args)

    return jax.shard_map(
        per_device,
        mesh=mesh,
        in_specs=(
            P("section", "blk", "head"),
            P("section", "blk", "head"),
            P("section", "blk", "head"),
            P("section", ("blk", "head"), None),
            P("section"),
        ),
        out_specs=(
            P("section", ("blk", "head"), None),
            P("section", ("blk", "head"), None),
            P("section", ("blk", "head"), None),
        ),
        check_vma=False,
    )
```

```python
import functools
import math

import jax
import jax.numpy as jnp
from jax import lax
from jax.experimental import pallas as pl
from jax.experimental.pallas import tpu as pltpu
from jax.sharding import PartitionSpec as P

HD = 128
LOG2E = math.log2(math.e)
MASKED = -1e30
NT = (((1,), (1,)), ((), ()))
VMEM_LIMIT = 60 * 2**20
BUSY, BRIEF = 40_000_000_000, 1


def cols(index):
    return pl.ds(pl.multiple_of(index * HD, HD), HD)


def run_copies(pairs, sems):
    copies = [pltpu.make_async_copy(src, dst, sems.at[i]) for i, (src, dst) in enumerate(pairs)]
    for copy in copies:
        copy.start()
    for copy in copies:
        copy.wait()


def run_staged(pairs, stage, sems):
    loads, stores = [], []
    for i, (src, dst) in enumerate(pairs):
        buf = stage.at[i, pl.ds(0, src.shape[0]), :]
        loads.append(pltpu.make_async_copy(src, buf, sems.at[0, i]))
        stores.append(pltpu.make_async_copy(buf, dst, sems.at[1, i]))
    for load in loads:
        load.start()
    for load, store in zip(loads, stores):
        load.wait()
        store.start()
    for store in stores:
        store.wait()


class Chain:
    def __init__(self, resident):
        self.resident = resident
        self.token = None

    def call(self, body, place, operands, out_shapes, aliases=None, **kwargs):
        any_space = pl.BlockSpec(memory_space=pl.ANY)
        in_hbm = pl.BlockSpec(memory_space=pltpu.HBM)
        spaces = [in_hbm if any(x is a for a in self.resident) else any_space for x in operands]
        n_in, n_out = len(operands), len(out_shapes)

        held = [] if self.token is None else [self.token]
        n_held = len(held)
        first_out = n_held + n_in + 1

        def whole(place_ref, *refs):
            outs, scratch = refs[first_out : first_out + n_out], refs[first_out + n_out :]
            body(place_ref, refs[n_held : n_held + n_in], outs, scratch)

        self.token, *outs = pl.pallas_call(
            whole,
            out_shape=(jax.ShapeDtypeStruct((8, HD), jnp.float32), *out_shapes),
            in_specs=[pl.BlockSpec(memory_space=pltpu.SMEM), *[any_space] * n_held, *spaces],
            out_specs=(any_space,) * (n_out + 1),
            input_output_aliases={i + 1 + n_held: o + 1 for i, o in (aliases or {}).items()},
            **kwargs,
        )(place, *held, *operands)
        return outs


def copy_kernel(chain, plan, count, rows, out_shapes, place, operands, name, aliases=None, weight=BUSY):
    def body(place_ref, ins, outs, scratch):
        run_staged(plan(place_ref, ins, outs), *scratch)

    moved = count * rows * HD * 2
    return chain.call(
        body,
        place,
        operands,
        out_shapes,
        aliases,
        scratch_shapes=[
            pltpu.VMEM((count, rows, HD), jnp.bfloat16),
            pltpu.SemaphoreType.DMA((2, count)),
        ],
        compiler_params=pltpu.CompilerParams(vmem_limit_bytes=VMEM_LIMIT),
        cost_estimate=pl.CostEstimate(flops=weight, bytes_accessed=1, transcendentals=0),
        name=name,
    )


class Layout:
    def __init__(self, rows, width, nb, nh):
        self.rows, self.nb, self.nh = rows, nb, nh
        self.heads = width // HD
        self.per = self.heads // nb
        self.nx = nb // 2
        self.part = rows // nh
        self.seq = rows * nb


def bf16(*shape):
    return jax.ShapeDtypeStruct(shape, jnp.bfloat16)


def prepare(tk, k_s, kt_s, ak_s, av_s):
    for t in range(k_s.shape[0] // tk):
        kt_s[t] = k_s[t * tk : (t + 1) * tk, :].T
    ak_s[...] = jnp.zeros_like(ak_s)
    av_s[...] = jnp.zeros_like(av_s)


def attention_body(lay, bq, tk, run2, place, q_s, k_s, v_s, g_s, dq_s, dk_s, dv_s, e_s, d_s, m_s, kt_s, ak_s, av_s, dqt_s, qw_s, kw_s):
    seq, rows = lay.seq, lay.rows
    nq, nt = seq // bq, seq // tk
    c = HD**-0.5 * LOG2E
    limit, blk = place[0], place[1]
    live = [jnp.clip(limit - (blk ^ k) * rows, 0, rows) for k in range(lay.nb)]
    full = limit >= seq

    @pl.when(jnp.logical_not(full))
    def _():
        for k in range(lay.nb):
            span = slice(k * rows, (k + 1) * rows)
            row = lax.broadcasted_iota(jnp.int32, (rows, HD), 0)
            zeros = jnp.zeros((rows, HD), jnp.bfloat16)
            g_s[span, :] = jnp.where(row < live[k], g_s[span, :], zeros)
            first = lax.broadcasted_iota(jnp.int32, (rows, HD), 1) == 0
            qw_s[span, :HD] = q_s[span, :]
            qw_s[span, HD:] = jnp.where(first, 1.0, 0.0).astype(jnp.bfloat16)
            kw_s[span, :HD] = k_s[span, :]
            kw_s[span, HD:] = jnp.where(first & (row >= live[k]), MASKED, 0.0).astype(jnp.bfloat16)

    def run(masked):
        q_in, k_in = (qw_s, kw_s) if masked else (q_s, k_s)

        def step(i, carry):
            off = pl.multiple_of(i * bq, bq)
            qb = q_s[pl.ds(off, bq), :]
            qa = q_in[pl.ds(off, bq), :]
            gb = g_s[pl.ds(off, bq), :]
            top = jnp.full((1, bq), 2 * MASKED, jnp.float32)
            total = jnp.zeros((1, bq), jnp.float32)
            dot = total
            for t in range(nt):
                span = slice(t * tk, (t + 1) * tk)
                s = lax.dot_general(k_in[span, :], qa, NT, preferred_element_type=jnp.float32) * c
                new = jnp.maximum(top, jnp.max(s, axis=0, keepdims=True))
                e = jnp.exp2(s - new)
                d = lax.dot_general(v_s[span, :], gb, NT, preferred_element_type=jnp.float32)
                e_s[span, :] = e
                d_s[span, :] = d
                m_s[t] = new
                fade = jnp.exp2(top - new)
                total = total * fade + jnp.sum(e, axis=0, keepdims=True)
                dot = dot * fade + jnp.sum(e * d, axis=0, keepdims=True)
                top = new
            delta = dot / total
            lse = top + jnp.log2(total)
            dqt_s[...] = jnp.zeros_like(dqt_s)

            def tiles(j, carry):
                sum_q = jnp.zeros((HD, bq), jnp.float32)
                for u in range(run2):
                    t = j * run2 + u
                    span = pl.ds(pl.multiple_of(t * tk, tk), tk)
                    p = e_s[span, :] * jnp.exp2(m_s[t] - lse)
                    ds = (p * (d_s[span, :] - delta)).astype(jnp.bfloat16)
                    pb = p.astype(jnp.bfloat16)
                    av_s[span, :] += jnp.dot(pb, gb, preferred_element_type=jnp.float32)
                    ak_s[span, :] += jnp.dot(ds, qb, preferred_element_type=jnp.float32)
                    sum_q += jnp.dot(kt_s[t], ds, preferred_element_type=jnp.float32)
                dqt_s[...] += sum_q
                return carry

            lax.fori_loop(0, nt // run2, tiles, 0)
            dq_s[pl.ds(off, bq), :] = (dqt_s[...] * HD**-0.5).T.astype(jnp.bfloat16)
            return carry

        lax.fori_loop(0, nq, step, 0)

    pl.when(full)(lambda: run(False))
    pl.when(jnp.logical_not(full))(lambda: run(True))
    dk_s[...] = (ak_s[...] * HD**-0.5).astype(jnp.bfloat16)
    dv_s[...] = av_s[...].astype(jnp.bfloat16)


def attention(chain, lay, place, sources, operands, name):
    seq, part = lay.seq, lay.part
    bq, tk = math.gcd(1024, seq), math.gcd(256, lay.rows)
    run2 = math.gcd(4, seq // tk)
    def body(place_ref, ins, outs, scratch):
        bufs, results, work, sems = scratch[:4], scratch[4:7], scratch[7:-1], scratch[-1]
        pairs, order = [], ([], [])
        for n, (buf, listing) in enumerate(zip(bufs, sources(place_ref, ins))):
            for start, size, src in listing:
                order[0 if n == 1 else 1].append(len(pairs))
                pairs.append((src, buf.at[pl.ds(start, size), :]))
        copies = [pltpu.make_async_copy(src, dst, sems.at[i]) for i, (src, dst) in enumerate(pairs)]
        for copy in copies:
            copy.start()
        for i in order[0]:
            copies[i].wait()
        prepare(tk, bufs[1], *work[3:6])
        for i in order[1]:
            copies[i].wait()
        attention_body(lay, bq, tk, run2, place_ref, *bufs, *results, *work)
        run_copies(
            [
                (
                    results[t].at[pl.ds((k * lay.nh + h) * part, part), :],
                    outs[0].at[h * lay.nb + (place_ref[1] ^ k), t],
                )
                for h in range(lay.nh)
                for k in range(lay.nb)
                for t in range(3)
            ],
            sems,
        )

    flops = 2 * seq * seq * HD
    vec = lambda *s: pltpu.VMEM(s, jnp.bfloat16)
    acc = lambda *s: pltpu.VMEM(s, jnp.float32)
    n_sems = 4 * lay.nb * lay.nh
    return chain.call(
        body,
        place,
        operands,
        [bf16(lay.nh * lay.nb, 3, part, HD)],
        scratch_shapes=[vec(seq, HD)] * 7
        + [acc(seq, bq), acc(seq, bq), acc(seq // tk, 1, bq), vec(seq // tk, HD, tk)]
        + [acc(seq, HD), acc(seq, HD), acc(HD, bq), vec(seq, 2 * HD), vec(seq, 2 * HD)]
        + [pltpu.SemaphoreType.DMA((n_sems,))],
        compiler_params=pltpu.CompilerParams(vmem_limit_bytes=VMEM_LIMIT),
        cost_estimate=pl.CostEstimate(flops=400_000_000_000, bytes_accessed=1, transcendentals=0),
        name=name,
    )


def split_heads_program(lay, query_states, key_states, value_states, grad_next, valid_count, sections):
    nb, nh, nx, per, part, rows, heads = lay.nb, lay.nh, lay.nx, lay.per, lay.part, lay.rows, lay.heads
    blk, head = lax.axis_index("blk"), lax.axis_index("head")
    place = jnp.stack([valid_count[0], blk, head]).astype(jnp.int32)
    qkv = [query_states, key_states, value_states]
    chain = Chain([*qkv, grad_next])

    def grad_rows(at, refs, i, dest):
        return [(pl.multiple_of((at[2] ^ kh) * part, part), part, refs[kh].at[i, dest]) for kh in range(nh)]

    def send_grads(group):
        def plan(at, ins, outs):
            pairs = []
            for kh in range(nh):
                for i, c in enumerate(group):
                    for o in range(nb):
                        src = ins[0].at[0, :, cols((at[2] ^ kh) * heads + o * per + c)]
                        pairs.append((src, outs[kh].at[i, o]))
            return pairs

        shape = bf16(len(group), nb, part, HD)
        count = nh * len(group) * nb
        packed = copy_kernel(
            chain, plan, count, part, [shape] * nh, place, [grad_next], f"pack_grads_{group[0]}",
            weight=BRIEF,
        )
        moved = []
        for kh in range(nh):
            route = [
                (s * nh + h, (s - 1) % sections * nh + (h ^ kh))
                for s in range(sections)
                for h in range(nh)
            ]
            moved.append(lax.ppermute(packed[kh], ("section", "head"), route))
        return {c: (moved, i) for i, c in enumerate(group)}

    def blk_send(x, k):
        return lax.ppermute(x, "blk", [(i, i ^ k) for i in range(nb)])

    def send_far(c, kx, tensors, grads, name):
        refs, slot = grads if grads else ([], 0)
        extra = 1 if grads else 0

        def plan(at, ins, outs):
            pairs = []
            for j in range(2):
                dest = at[1] ^ (2 * kx + j)
                for t in range(len(tensors)):
                    pairs.append((ins[t].at[0, :, cols(dest * per + c)], outs[0].at[t, j]))
                if extra:
                    for start, size, src in grad_rows(at, ins[len(tensors) :], slot, dest):
                        pairs.append((src, outs[0].at[len(tensors), j, pl.ds(start, size), :]))
            return pairs

        n = 2 * (len(tensors) + extra * nh)
        shape = bf16(len(tensors) + extra, 2, rows, HD)
        weight = BRIEF if c == 0 or (c == 1 and tensors) else BUSY
        packed = copy_kernel(chain, plan, n, rows, [shape], place, [*tensors, *refs], name, weight=weight)
        return blk_send(packed[0], 2 * kx)

    def send_near(c, grads, far):
        refs, slot = grads

        def plan(at, ins, outs):
            pairs = []
            dest = at[1] ^ 1
            for t in range(3):
                pairs.append((ins[t].at[0, :, cols(dest * per + c)], outs[0].at[t, 0]))
            for start, size, src in grad_rows(at, ins[3 : 3 + nh], slot, dest):
                pairs.append((src, outs[0].at[3, 0, pl.ds(start, size), :]))
            rest = iter(ins[3 + nh :])
            for kx in range(1, nx):
                for begin, count, _ in far[kx]:
                    ref = next(rest)
                    for t in range(count):
                        pairs.append((ref.at[t, 1], outs[0].at[begin + t, kx]))
            return pairs

        arrays = [a for kx in range(1, nx) for _, _, a in far[kx]]
        n = 3 + nh + 4 * (nx - 1)
        packed = copy_kernel(
            chain, plan, n, rows, [bf16(4, nx, rows, HD)], place, [*qkv, *refs, *arrays], f"pack_near_{c}"
        )
        return blk_send(packed[0], 1)

    def attend(c, grads, far, near, after):
        refs, slot = grads

        def sources(at, ins):
            near_ref = ins[3 + nh]
            far_refs = iter(ins[4 + nh :])
            listing = [[], [], [], []]
            for t in range(3):
                listing[t].append((0, rows, ins[t].at[0, :, cols(at[1] * per + c)]))
            listing[3].extend(grad_rows(at, ins[3 : 3 + nh], slot, at[1]))
            for kx in range(nx):
                for t in range(4):
                    listing[t].append(((2 * kx + 1) * rows, rows, near_ref.at[t, kx]))
            for kx in range(1, nx):
                for begin, count, _ in far[kx]:
                    ref = next(far_refs)
                    for t in range(count):
                        listing[begin + t].append((2 * kx * rows, rows, ref.at[t, 0]))
            return listing

        arrays = [a for kx in range(1, nx) for _, _, a in far[kx]]
        sent = attention(chain, lay, place, sources, [*qkv, *refs, near, *arrays, *after], f"attention_{c}")
        return lax.all_to_all(sent[0], ("head", "blk"), split_axis=0, concat_axis=0, tiled=True)

    def place_outputs(c, got, outs):
        def plan(at, ins, out_refs):
            return [
                (ins[0].at[h * nb + o, t], out_refs[t].at[0, :, cols(h * heads + o * per + c)])
                for h in range(nh)
                for o in range(nb)
                for t in range(3)
            ]

        shape = bf16(1, part, nh * heads * HD)
        aliases = {1 + t: t for t in range(3)} if outs else None
        operands = [got, *(outs or [])]
        return copy_kernel(
            chain, plan, 3 * nh * nb, part, [shape] * 3, place, operands, f"unpack_{c}", aliases,
            weight=BUSY if c < per - 3 else BRIEF,
        )

    fars = range(1, nx)
    far, near, grads, got, outs = {}, {}, {}, {}, None

    def far_tensors(c, tensors, cotangent, first):
        for kx in fars:
            name = f"pack_far_{c}_{kx}_{first}"
            count = len(tensors) + (1 if cotangent else 0)
            x = send_far(c, kx, tensors, grads[c] if cotangent else None, name)
            far.setdefault(c, {}).setdefault(kx, []).append((first, count, x))

    far_tensors(0, qkv, False, 0)
    grads.update(send_grads([0]))
    if per > 1:
        grads.update(send_grads([1]))
        if per > 2:
            grads.update(send_grads(list(range(2, per))))
        far_tensors(1, qkv, False, 0)
    far_tensors(0, [], True, 3)
    near[0] = send_near(0, grads[0], far[0])
    if per > 1:
        far_tensors(1, [], True, 3)
    if per > 2:
        far_tensors(2, qkv, False, 0)
    for c in range(per):
        late = [got[c - 2]] if c > 1 and c == per - 1 else []
        got[c] = attend(c, grads[c], far[c], near[c], late)
        if c + 1 < per:
            near[c + 1] = send_near(c + 1, grads[c + 1], far[c + 1])
        if c + 2 < per and c == 0:
            far_tensors(2, [], True, 3)
        if c + 3 < per:
            far_tensors(c + 3, qkv, True, 0)
        if 0 < c < per - 2:
            outs = place_outputs(c - 1, got[c - 1], outs)
    for c in range(max(per - 3, 0), per):
        outs = place_outputs(c, got[c], outs)
    return tuple(outs)


def shifted(x, axis, by):
    peers = lax.axis_size(axis)
    return lax.ppermute(x, axis, [(i, (i + by) % peers) for i in range(peers)])


def masked_scores(query_block, key_block, key_positions, limit):
    scores = jnp.einsum(
        "qhd,khd->hqk", query_block, key_block, preferred_element_type=jnp.float32
    ) * HD ** (-0.5)
    return jnp.where(key_positions[None, None, :] < limit, scores, -jnp.inf)


def gathered_program(query_states, key_states, value_states, grad_next, valid_count):
    scale = HD ** (-0.5)
    blk_index = lax.axis_index("blk")
    incoming = shifted(grad_next, "section", -1)
    grads = lax.all_to_all(incoming, "head", split_axis=2, concat_axis=1, tiled=True)
    shard_rows = query_states.shape[1]
    width = query_states.shape[2]
    local_heads = width // HD
    limit = valid_count[0]
    own_positions = blk_index * shard_rows + jnp.arange(shard_rows, dtype=jnp.int32)
    grads = jnp.where((own_positions < limit)[None, :, None], grads, jnp.zeros_like(grads))
    query_heads = query_states[0].reshape(shard_rows, local_heads, HD)
    grad_heads = grads[0].reshape(shard_rows, local_heads, HD)
    gathered_keys, gathered_values = (
        lax.all_gather(key_states, "blk", axis=1, tiled=True),
        lax.all_gather(value_states, "blk", axis=1, tiled=True),
    )
    key_count = gathered_keys.shape[1]
    block_rows = math.gcd(512, key_count)
    block_count = key_count // block_rows
    key_blocks = gathered_keys[0].reshape(block_count, block_rows, local_heads, HD)
    value_blocks = gathered_values[0].reshape(block_count, block_rows, local_heads, HD)
    position_blocks = jnp.arange(key_count, dtype=jnp.int32).reshape(block_count, block_rows)

    def forward_step(carry, block):
        run_max, run_sum, run_dot = carry
        key_block, value_block, key_pos = block
        scores = masked_scores(query_heads, key_block, key_pos, limit)
        grad_probs = jnp.einsum(
            "qhd,khd->hqk", grad_heads, value_block, preferred_element_type=jnp.float32
        )
        new_max = jnp.maximum(run_max, jnp.max(scores, axis=2))
        factor = jnp.exp(run_max - new_max)
        weights = jnp.exp(scores - new_max[:, :, None])
        run_sum = run_sum * factor + jnp.sum(weights, axis=2)
        run_dot = run_dot * factor + jnp.sum(weights * grad_probs, axis=2)
        return ((new_max, run_sum, run_dot), None)

    start_max = jnp.full((local_heads, shard_rows), -jnp.inf, jnp.float32)
    start_zero = jnp.zeros((local_heads, shard_rows), jnp.float32)
    (run_max, run_sum, run_dot), _ = lax.scan(
        forward_step,
        (start_max, start_zero, start_zero),
        (key_blocks, value_blocks, position_blocks),
    )
    log_total = run_max + jnp.log(run_sum)
    delta = run_dot / run_sum

    def block_terms(
        query_block, grad_block, key_block, value_block, key_pos, block_log, block_delta
    ):
        scores = masked_scores(query_block, key_block, key_pos, limit)
        probs = jnp.exp(scores - block_log[:, :, None])
        grad_probs = jnp.einsum(
            "qhd,khd->hqk", grad_block, value_block, preferred_element_type=jnp.float32
        )
        grad_scores = (probs * (grad_probs - block_delta[:, :, None])).astype(jnp.bfloat16)
        return (probs.astype(jnp.bfloat16), grad_scores)

    zero_rows = jnp.zeros((shard_rows, local_heads, HD), jnp.float32)

    def query_step(grad_q, block):
        key_block, value_block, key_pos = block
        prob_low, grad_scores = block_terms(
            query_heads, grad_heads, key_block, value_block, key_pos, log_total, delta
        )
        grad_q = (
            grad_q
            + jnp.einsum("hqk,khd->qhd", grad_scores, key_block, preferred_element_type=jnp.float32)
            * scale
        )
        return (grad_q, None)

    grad_q, _ = lax.scan(query_step, zero_rows, (key_blocks, value_blocks, position_blocks))
    all_log, all_delta = (
        lax.all_gather(log_total.T[None], "blk", axis=1, tiled=True),
        lax.all_gather(delta.T[None], "blk", axis=1, tiled=True),
    )
    key_heads = key_states[0].reshape(shard_rows, local_heads, HD)
    value_heads = value_states[0].reshape(shard_rows, local_heads, HD)
    piece_queries = lax.all_gather(query_states, "blk", axis=1, tiled=True)
    piece_grads = lax.all_gather(grads, "blk", axis=1, tiled=True)
    piece_rows = piece_queries.shape[1]
    sub_rows = math.gcd(shard_rows, piece_rows)
    sub_count = piece_rows // sub_rows
    piece_log = all_log[0]
    piece_delta = all_delta[0]
    sub_queries = piece_queries[0].reshape(sub_count, sub_rows, local_heads, HD)
    sub_grads = piece_grads[0].reshape(sub_count, sub_rows, local_heads, HD)
    sub_log = piece_log.reshape(sub_count, sub_rows, local_heads)
    sub_delta = piece_delta.reshape(sub_count, sub_rows, local_heads)

    def sub_step(accum, sub):
        acc_k, acc_v = accum
        query_block, grad_block, block_log, block_delta = sub
        prob_low, grad_scores = block_terms(
            query_block,
            grad_block,
            key_heads,
            value_heads,
            own_positions,
            block_log.T,
            block_delta.T,
        )
        acc_v = acc_v + jnp.einsum(
            "hqk,qhd->khd", prob_low, grad_block, preferred_element_type=jnp.float32
        )
        acc_k = (
            acc_k
            + jnp.einsum(
                "hqk,qhd->khd", grad_scores, query_block, preferred_element_type=jnp.float32
            )
            * scale
        )
        return ((acc_k, acc_v), None)

    result, _ = lax.scan(
        sub_step, (zero_rows, zero_rows), (sub_queries, sub_grads, sub_log, sub_delta)
    )
    grad_k, grad_v = result
    grad_q_low = grad_q.reshape(1, shard_rows, width).astype(jnp.bfloat16)
    grad_k_low = grad_k.reshape(1, shard_rows, width).astype(jnp.bfloat16)
    grad_v_low = grad_v.reshape(1, shard_rows, width).astype(jnp.bfloat16)
    grad_query, grad_key, grad_value = (
        lax.all_to_all(grad_q_low, "head", split_axis=1, concat_axis=2, tiled=True),
        lax.all_to_all(grad_k_low, "head", split_axis=1, concat_axis=2, tiled=True),
        lax.all_to_all(grad_v_low, "head", split_axis=1, concat_axis=2, tiled=True),
    )
    return (grad_query, grad_key, grad_value)


def solution(mesh):
    sections, nh, nb = (mesh.shape[a] for a in ("section", "head", "blk"))

    def per_device(query_states, key_states, value_states, grad_next, valid_count):
        lay = Layout(query_states.shape[1], query_states.shape[2], nb, nh)
        powers = nb & (nb - 1) == 0 and nh & (nh - 1) == 0 and nb > 1
        args = (query_states, key_states, value_states, grad_next, valid_count)
        if powers and lay.heads % nb == 0 and lay.part % 16 == 0:
            return split_heads_program(lay, *args, sections)
        return gathered_program(*args)

    return jax.shard_map(
        per_device,
        mesh=mesh,
        in_specs=(
            P("section", "blk", "head"),
            P("section", "blk", "head"),
            P("section", "blk", "head"),
            P("section", ("blk", "head"), None),
            P("section"),
        ),
        out_specs=(
            P("section", ("blk", "head"), None),
            P("section", ("blk", "head"), None),
            P("section", ("blk", "head"), None),
        ),
        check_vma=False,
    )
```

```python
import functools
import math

import jax
import jax.numpy as jnp
from jax import lax
from jax.experimental import pallas as pl
from jax.experimental.pallas import tpu as pltpu
from jax.sharding import PartitionSpec as P

HD = 128
LOG2E = math.log2(math.e)
MASKED = -1e30
NT = (((1,), (1,)), ((), ()))
VMEM_LIMIT = 63 * 2**20
BUSY, BRIEF = 40_000_000_000, 1


def cols(index):
    return pl.ds(pl.multiple_of(index * HD, HD), HD)


def run_copies(pairs, sems):
    copies = [pltpu.make_async_copy(src, dst, sems.at[i]) for i, (src, dst) in enumerate(pairs)]
    for copy in copies:
        copy.start()
    for copy in copies:
        copy.wait()


def run_staged(pairs, stage, sems):
    loads, stores = [], []
    for i, (src, dst) in enumerate(pairs):
        buf = stage.at[i, pl.ds(0, src.shape[0]), :]
        loads.append(pltpu.make_async_copy(src, buf, sems.at[0, i]))
        stores.append(pltpu.make_async_copy(buf, dst, sems.at[1, i]))
    for load in loads:
        load.start()
    for load, store in zip(loads, stores):
        load.wait()
        store.start()
    for store in stores:
        store.wait()


class Chain:
    def __init__(self, resident):
        self.resident = resident
        self.token = None

    def call(self, body, place, operands, out_shapes, aliases=None, **kwargs):
        any_space = pl.BlockSpec(memory_space=pl.ANY)
        in_hbm = pl.BlockSpec(memory_space=pltpu.HBM)
        spaces = [in_hbm if any(x is a for a in self.resident) else any_space for x in operands]
        n_in, n_out = len(operands), len(out_shapes)

        held = [] if self.token is None else [self.token]
        n_held = len(held)
        first_out = n_held + n_in + 1

        def whole(place_ref, *refs):
            outs, scratch = refs[first_out : first_out + n_out], refs[first_out + n_out :]
            body(place_ref, refs[n_held : n_held + n_in], outs, scratch)

        self.token, *outs = pl.pallas_call(
            whole,
            out_shape=(jax.ShapeDtypeStruct((8, HD), jnp.float32), *out_shapes),
            in_specs=[pl.BlockSpec(memory_space=pltpu.SMEM), *[any_space] * n_held, *spaces],
            out_specs=(any_space,) * (n_out + 1),
            input_output_aliases={i + 1 + n_held: o + 1 for i, o in (aliases or {}).items()},
            **kwargs,
        )(place, *held, *operands)
        return outs


def copy_kernel(chain, plan, count, rows, out_shapes, place, operands, name, aliases=None, weight=BUSY):
    def body(place_ref, ins, outs, scratch):
        run_staged(plan(place_ref, ins, outs), *scratch)

    moved = count * rows * HD * 2
    return chain.call(
        body,
        place,
        operands,
        out_shapes,
        aliases,
        scratch_shapes=[
            pltpu.VMEM((count, rows, HD), jnp.bfloat16),
            pltpu.SemaphoreType.DMA((2, count)),
        ],
        compiler_params=pltpu.CompilerParams(vmem_limit_bytes=VMEM_LIMIT),
        cost_estimate=pl.CostEstimate(flops=weight, bytes_accessed=1, transcendentals=0),
        name=name,
    )


class Layout:
    def __init__(self, rows, width, nb, nh):
        self.rows, self.nb, self.nh = rows, nb, nh
        self.heads = width // HD
        self.per = self.heads // nb
        self.nx = nb // 2
        self.part = rows // nh
        self.seq = rows * nb


def bf16(*shape):
    return jax.ShapeDtypeStruct(shape, jnp.bfloat16)


def prepare(tk, k_s, kt_s, ak_s, av_s):
    for t in range(k_s.shape[0] // tk):
        kt_s[t] = k_s[t * tk : (t + 1) * tk, :].T
    ak_s[...] = jnp.zeros_like(ak_s)
    av_s[...] = jnp.zeros_like(av_s)


def attention_body(lay, bq, tk, run2, place, q_s, k_s, v_s, g_s, dq_s, dk_s, dv_s, e_s, d_s, m_s, kt_s, ak_s, av_s, dqt_s, qw_s, kw_s):
    seq, rows = lay.seq, lay.rows
    nq, nt = seq // bq, seq // tk
    c = HD**-0.5 * LOG2E
    limit, blk = place[0], place[1]
    live = [jnp.clip(limit - (blk ^ k) * rows, 0, rows) for k in range(lay.nb)]
    full = limit >= seq

    @pl.when(jnp.logical_not(full))
    def _():
        for k in range(lay.nb):
            span = slice(k * rows, (k + 1) * rows)
            row = lax.broadcasted_iota(jnp.int32, (rows, HD), 0)
            zeros = jnp.zeros((rows, HD), jnp.bfloat16)
            g_s[span, :] = jnp.where(row < live[k], g_s[span, :], zeros)
            first = lax.broadcasted_iota(jnp.int32, (rows, HD), 1) == 0
            qw_s[span, :HD] = q_s[span, :]
            qw_s[span, HD:] = jnp.where(first, 1.0, 0.0).astype(jnp.bfloat16)
            kw_s[span, :HD] = k_s[span, :]
            kw_s[span, HD:] = jnp.where(first & (row >= live[k]), MASKED, 0.0).astype(jnp.bfloat16)

    def run(masked):
        q_in, k_in = (qw_s, kw_s) if masked else (q_s, k_s)

        def step(i, carry):
            off = pl.multiple_of(i * bq, bq)
            qb = q_s[pl.ds(off, bq), :]
            qa = q_in[pl.ds(off, bq), :]
            gb = g_s[pl.ds(off, bq), :]
            top = jnp.full((1, bq), 2 * MASKED, jnp.float32)
            total = jnp.zeros((1, bq), jnp.float32)
            dot = total
            for t in range(nt):
                span = slice(t * tk, (t + 1) * tk)
                s = lax.dot_general(k_in[span, :], qa, NT, preferred_element_type=jnp.float32) * c
                new = jnp.maximum(top, jnp.max(s, axis=0, keepdims=True))
                e = jnp.exp2(s - new)
                d = lax.dot_general(v_s[span, :], gb, NT, preferred_element_type=jnp.float32)
                e_s[span, :] = e
                d_s[span, :] = d
                m_s[t] = new
                fade = jnp.exp2(top - new)
                total = total * fade + jnp.sum(e, axis=0, keepdims=True)
                dot = dot * fade + jnp.sum(e * d, axis=0, keepdims=True)
                top = new
            delta = dot / total
            lse = top + jnp.log2(total)
            dqt_s[...] = jnp.zeros_like(dqt_s)

            def tiles(j, carry):
                sum_q = jnp.zeros((HD, bq), jnp.float32)
                for u in range(run2):
                    t = j * run2 + u
                    span = pl.ds(pl.multiple_of(t * tk, tk), tk)
                    p = e_s[span, :] * jnp.exp2(m_s[t] - lse)
                    ds = (p * (d_s[span, :] - delta)).astype(jnp.bfloat16)
                    pb = p.astype(jnp.bfloat16)
                    av_s[span, :] += jnp.dot(pb, gb, preferred_element_type=jnp.float32)
                    ak_s[span, :] += jnp.dot(ds, qb, preferred_element_type=jnp.float32)
                    sum_q += jnp.dot(kt_s[t], ds, preferred_element_type=jnp.float32)
                dqt_s[...] += sum_q
                return carry

            lax.fori_loop(0, nt // run2, tiles, 0)
            dq_s[pl.ds(off, bq), :] = (dqt_s[...] * HD**-0.5).T.astype(jnp.bfloat16)
            return carry

        lax.fori_loop(0, nq, step, 0)

    pl.when(full)(lambda: run(False))
    pl.when(jnp.logical_not(full))(lambda: run(True))
    dk_s[...] = (ak_s[...] * HD**-0.5).astype(jnp.bfloat16)
    dv_s[...] = av_s[...].astype(jnp.bfloat16)


def attention(chain, lay, place, sources, operands, name):
    seq, part = lay.seq, lay.part
    bq, tk = math.gcd(1024, seq), math.gcd(256, lay.rows)
    run2 = math.gcd(4, seq // tk)
    def body(place_ref, ins, outs, scratch):
        bufs, results, work, sems = scratch[:4], scratch[4:7], scratch[7:-1], scratch[-1]
        pairs, order = [], ([], [])
        for n, (buf, listing) in enumerate(zip(bufs, sources(place_ref, ins))):
            for start, size, src in listing:
                order[0 if n == 1 else 1].append(len(pairs))
                pairs.append((src, buf.at[pl.ds(start, size), :]))
        copies = [pltpu.make_async_copy(src, dst, sems.at[i]) for i, (src, dst) in enumerate(pairs)]
        for copy in copies:
            copy.start()
        for i in order[0]:
            copies[i].wait()
        prepare(tk, bufs[1], *work[3:6])
        for i in order[1]:
            copies[i].wait()
        attention_body(lay, bq, tk, run2, place_ref, *bufs, *results, *work)
        run_copies(
            [
                (
                    results[t].at[pl.ds((k * lay.nh + h) * part, part), :],
                    outs[0].at[h * lay.nb + (place_ref[1] ^ k), t],
                )
                for h in range(lay.nh)
                for k in range(lay.nb)
                for t in range(3)
            ],
            sems,
        )

    flops = 2 * seq * seq * HD
    vec = lambda *s: pltpu.VMEM(s, jnp.bfloat16)
    acc = lambda *s: pltpu.VMEM(s, jnp.float32)
    n_sems = 4 * lay.nb * lay.nh
    return chain.call(
        body,
        place,
        operands,
        [bf16(lay.nh * lay.nb, 3, part, HD)],
        scratch_shapes=[vec(seq, HD)] * 7
        + [acc(seq, bq), acc(seq, bq), acc(seq // tk, 1, bq), vec(seq // tk, HD, tk)]
        + [acc(seq, HD), acc(seq, HD), acc(HD, bq), vec(seq, 2 * HD), vec(seq, 2 * HD)]
        + [pltpu.SemaphoreType.DMA((n_sems,))],
        compiler_params=pltpu.CompilerParams(vmem_limit_bytes=VMEM_LIMIT),
        cost_estimate=pl.CostEstimate(flops=400_000_000_000, bytes_accessed=1, transcendentals=0),
        name=name,
    )


def split_heads_program(lay, query_states, key_states, value_states, grad_next, valid_count, sections):
    nb, nh, nx, per, part, rows, heads = lay.nb, lay.nh, lay.nx, lay.per, lay.part, lay.rows, lay.heads
    blk, head = lax.axis_index("blk"), lax.axis_index("head")
    place = jnp.stack([valid_count[0], blk, head]).astype(jnp.int32)
    qkv = [query_states, key_states, value_states]
    chain = Chain([*qkv, grad_next])

    def grad_rows(at, refs, i, dest):
        return [(pl.multiple_of((at[2] ^ kh) * part, part), part, refs[kh].at[i, dest]) for kh in range(nh)]

    def send_grads(group):
        def plan(at, ins, outs):
            pairs = []
            for kh in range(nh):
                for i, c in enumerate(group):
                    for o in range(nb):
                        src = ins[0].at[0, :, cols((at[2] ^ kh) * heads + o * per + c)]
                        pairs.append((src, outs[kh].at[i, o]))
            return pairs

        shape = bf16(len(group), nb, part, HD)
        count = nh * len(group) * nb
        packed = copy_kernel(
            chain, plan, count, part, [shape] * nh, place, [grad_next], f"pack_grads_{group[0]}",
            weight=BRIEF,
        )
        moved = []
        for kh in range(nh):
            route = [
                (s * nh + h, (s - 1) % sections * nh + (h ^ kh))
                for s in range(sections)
                for h in range(nh)
            ]
            moved.append(lax.ppermute(packed[kh], ("section", "head"), route))
        return {c: (moved, i) for i, c in enumerate(group)}

    def blk_send(x, k):
        return lax.ppermute(x, "blk", [(i, i ^ k) for i in range(nb)])

    def send_far(c, kx, tensors, grads, name):
        refs, slot = grads if grads else ([], 0)
        extra = 1 if grads else 0

        def plan(at, ins, outs):
            pairs = []
            for j in range(2):
                dest = at[1] ^ (2 * kx + j)
                for t in range(len(tensors)):
                    pairs.append((ins[t].at[0, :, cols(dest * per + c)], outs[0].at[t, j]))
                if extra:
                    for start, size, src in grad_rows(at, ins[len(tensors) :], slot, dest):
                        pairs.append((src, outs[0].at[len(tensors), j, pl.ds(start, size), :]))
            return pairs

        n = 2 * (len(tensors) + extra * nh)
        shape = bf16(len(tensors) + extra, 2, rows, HD)
        weight = BRIEF if c == 0 or (c == 1 and tensors) else BUSY
        packed = copy_kernel(chain, plan, n, rows, [shape], place, [*tensors, *refs], name, weight=weight)
        return blk_send(packed[0], 2 * kx)

    def send_near(c, grads, far):
        refs, slot = grads

        def plan(at, ins, outs):
            pairs = []
            dest = at[1] ^ 1
            for t in range(3):
                pairs.append((ins[t].at[0, :, cols(dest * per + c)], outs[0].at[t, 0]))
            for start, size, src in grad_rows(at, ins[3 : 3 + nh], slot, dest):
                pairs.append((src, outs[0].at[3, 0, pl.ds(start, size), :]))
            rest = iter(ins[3 + nh :])
            for kx in range(1, nx):
                for begin, count, _ in far[kx]:
                    ref = next(rest)
                    for t in range(count):
                        pairs.append((ref.at[t, 1], outs[0].at[begin + t, kx]))
            return pairs

        arrays = [a for kx in range(1, nx) for _, _, a in far[kx]]
        n = 3 + nh + 4 * (nx - 1)
        packed = copy_kernel(
            chain, plan, n, rows, [bf16(4, nx, rows, HD)], place, [*qkv, *refs, *arrays], f"pack_near_{c}"
        )
        return blk_send(packed[0], 1)

    def attend(c, grads, far, near, after):
        refs, slot = grads

        def sources(at, ins):
            near_ref = ins[3 + nh]
            far_refs = iter(ins[4 + nh :])
            listing = [[], [], [], []]
            for t in range(3):
                listing[t].append((0, rows, ins[t].at[0, :, cols(at[1] * per + c)]))
            listing[3].extend(grad_rows(at, ins[3 : 3 + nh], slot, at[1]))
            for kx in range(nx):
                for t in range(4):
                    listing[t].append(((2 * kx + 1) * rows, rows, near_ref.at[t, kx]))
            for kx in range(1, nx):
                for begin, count, _ in far[kx]:
                    ref = next(far_refs)
                    for t in range(count):
                        listing[begin + t].append((2 * kx * rows, rows, ref.at[t, 0]))
            return listing

        arrays = [a for kx in range(1, nx) for _, _, a in far[kx]]
        sent = attention(chain, lay, place, sources, [*qkv, *refs, near, *arrays, *after], f"attention_{c}")
        return lax.all_to_all(sent[0], ("head", "blk"), split_axis=0, concat_axis=0, tiled=True)

    def place_outputs(c, got, outs):
        def plan(at, ins, out_refs):
            return [
                (ins[0].at[h * nb + o, t], out_refs[t].at[0, :, cols(h * heads + o * per + c)])
                for h in range(nh)
                for o in range(nb)
                for t in range(3)
            ]

        shape = bf16(1, part, nh * heads * HD)
        aliases = {1 + t: t for t in range(3)} if outs else None
        operands = [got, *(outs or [])]
        return copy_kernel(
            chain, plan, 3 * nh * nb, part, [shape] * 3, place, operands, f"unpack_{c}", aliases,
            weight=BUSY if c < per - 3 else BRIEF,
        )

    fars = range(1, nx)
    far, near, grads, got, outs = {}, {}, {}, {}, None

    def far_tensors(c, tensors, cotangent, first):
        for kx in fars:
            name = f"pack_far_{c}_{kx}_{first}"
            count = len(tensors) + (1 if cotangent else 0)
            x = send_far(c, kx, tensors, grads[c] if cotangent else None, name)
            far.setdefault(c, {}).setdefault(kx, []).append((first, count, x))

    far_tensors(0, qkv, False, 0)
    grads.update(send_grads([0]))
    if per > 1:
        grads.update(send_grads([1]))
        if per > 2:
            grads.update(send_grads(list(range(2, per))))
        far_tensors(1, qkv, False, 0)
    far_tensors(0, [], True, 3)
    near[0] = send_near(0, grads[0], far[0])
    if per > 1:
        far_tensors(1, [], True, 3)
    if per > 2:
        far_tensors(2, qkv, False, 0)
    for c in range(per):
        late = [got[c - 2]] if c > 1 and c == per - 1 else []
        got[c] = attend(c, grads[c], far[c], near[c], late)
        if c + 1 < per:
            near[c + 1] = send_near(c + 1, grads[c + 1], far[c + 1])
        if c + 2 < per and c == 0:
            far_tensors(2, [], True, 3)
        if c + 3 < per:
            far_tensors(c + 3, qkv, True, 0)
        if 0 < c < per - 2:
            outs = place_outputs(c - 1, got[c - 1], outs)
    for c in range(max(per - 3, 0), per):
        outs = place_outputs(c, got[c], outs)
    return tuple(outs)


def shifted(x, axis, by):
    peers = lax.axis_size(axis)
    return lax.ppermute(x, axis, [(i, (i + by) % peers) for i in range(peers)])


def masked_scores(query_block, key_block, key_positions, limit):
    scores = jnp.einsum(
        "qhd,khd->hqk", query_block, key_block, preferred_element_type=jnp.float32
    ) * HD ** (-0.5)
    return jnp.where(key_positions[None, None, :] < limit, scores, -jnp.inf)


def gathered_program(query_states, key_states, value_states, grad_next, valid_count):
    scale = HD ** (-0.5)
    blk_index = lax.axis_index("blk")
    incoming = shifted(grad_next, "section", -1)
    grads = lax.all_to_all(incoming, "head", split_axis=2, concat_axis=1, tiled=True)
    shard_rows = query_states.shape[1]
    width = query_states.shape[2]
    local_heads = width // HD
    limit = valid_count[0]
    own_positions = blk_index * shard_rows + jnp.arange(shard_rows, dtype=jnp.int32)
    grads = jnp.where((own_positions < limit)[None, :, None], grads, jnp.zeros_like(grads))
    query_heads = query_states[0].reshape(shard_rows, local_heads, HD)
    grad_heads = grads[0].reshape(shard_rows, local_heads, HD)
    gathered_keys, gathered_values = (
        lax.all_gather(key_states, "blk", axis=1, tiled=True),
        lax.all_gather(value_states, "blk", axis=1, tiled=True),
    )
    key_count = gathered_keys.shape[1]
    block_rows = math.gcd(512, key_count)
    block_count = key_count // block_rows
    key_blocks = gathered_keys[0].reshape(block_count, block_rows, local_heads, HD)
    value_blocks = gathered_values[0].reshape(block_count, block_rows, local_heads, HD)
    position_blocks = jnp.arange(key_count, dtype=jnp.int32).reshape(block_count, block_rows)

    def forward_step(carry, block):
        run_max, run_sum, run_dot = carry
        key_block, value_block, key_pos = block
        scores = masked_scores(query_heads, key_block, key_pos, limit)
        grad_probs = jnp.einsum(
            "qhd,khd->hqk", grad_heads, value_block, preferred_element_type=jnp.float32
        )
        new_max = jnp.maximum(run_max, jnp.max(scores, axis=2))
        factor = jnp.exp(run_max - new_max)
        weights = jnp.exp(scores - new_max[:, :, None])
        run_sum = run_sum * factor + jnp.sum(weights, axis=2)
        run_dot = run_dot * factor + jnp.sum(weights * grad_probs, axis=2)
        return ((new_max, run_sum, run_dot), None)

    start_max = jnp.full((local_heads, shard_rows), -jnp.inf, jnp.float32)
    start_zero = jnp.zeros((local_heads, shard_rows), jnp.float32)
    (run_max, run_sum, run_dot), _ = lax.scan(
        forward_step,
        (start_max, start_zero, start_zero),
        (key_blocks, value_blocks, position_blocks),
    )
    log_total = run_max + jnp.log(run_sum)
    delta = run_dot / run_sum

    def block_terms(
        query_block, grad_block, key_block, value_block, key_pos, block_log, block_delta
    ):
        scores = masked_scores(query_block, key_block, key_pos, limit)
        probs = jnp.exp(scores - block_log[:, :, None])
        grad_probs = jnp.einsum(
            "qhd,khd->hqk", grad_block, value_block, preferred_element_type=jnp.float32
        )
        grad_scores = (probs * (grad_probs - block_delta[:, :, None])).astype(jnp.bfloat16)
        return (probs.astype(jnp.bfloat16), grad_scores)

    zero_rows = jnp.zeros((shard_rows, local_heads, HD), jnp.float32)

    def query_step(grad_q, block):
        key_block, value_block, key_pos = block
        prob_low, grad_scores = block_terms(
            query_heads, grad_heads, key_block, value_block, key_pos, log_total, delta
        )
        grad_q = (
            grad_q
            + jnp.einsum("hqk,khd->qhd", grad_scores, key_block, preferred_element_type=jnp.float32)
            * scale
        )
        return (grad_q, None)

    grad_q, _ = lax.scan(query_step, zero_rows, (key_blocks, value_blocks, position_blocks))
    all_log, all_delta = (
        lax.all_gather(log_total.T[None], "blk", axis=1, tiled=True),
        lax.all_gather(delta.T[None], "blk", axis=1, tiled=True),
    )
    key_heads = key_states[0].reshape(shard_rows, local_heads, HD)
    value_heads = value_states[0].reshape(shard_rows, local_heads, HD)
    piece_queries = lax.all_gather(query_states, "blk", axis=1, tiled=True)
    piece_grads = lax.all_gather(grads, "blk", axis=1, tiled=True)
    piece_rows = piece_queries.shape[1]
    sub_rows = math.gcd(shard_rows, piece_rows)
    sub_count = piece_rows // sub_rows
    piece_log = all_log[0]
    piece_delta = all_delta[0]
    sub_queries = piece_queries[0].reshape(sub_count, sub_rows, local_heads, HD)
    sub_grads = piece_grads[0].reshape(sub_count, sub_rows, local_heads, HD)
    sub_log = piece_log.reshape(sub_count, sub_rows, local_heads)
    sub_delta = piece_delta.reshape(sub_count, sub_rows, local_heads)

    def sub_step(accum, sub):
        acc_k, acc_v = accum
        query_block, grad_block, block_log, block_delta = sub
        prob_low, grad_scores = block_terms(
            query_block,
            grad_block,
            key_heads,
            value_heads,
            own_positions,
            block_log.T,
            block_delta.T,
        )
        acc_v = acc_v + jnp.einsum(
            "hqk,qhd->khd", prob_low, grad_block, preferred_element_type=jnp.float32
        )
        acc_k = (
            acc_k
            + jnp.einsum(
                "hqk,qhd->khd", grad_scores, query_block, preferred_element_type=jnp.float32
            )
            * scale
        )
        return ((acc_k, acc_v), None)

    result, _ = lax.scan(
        sub_step, (zero_rows, zero_rows), (sub_queries, sub_grads, sub_log, sub_delta)
    )
    grad_k, grad_v = result
    grad_q_low = grad_q.reshape(1, shard_rows, width).astype(jnp.bfloat16)
    grad_k_low = grad_k.reshape(1, shard_rows, width).astype(jnp.bfloat16)
    grad_v_low = grad_v.reshape(1, shard_rows, width).astype(jnp.bfloat16)
    grad_query, grad_key, grad_value = (
        lax.all_to_all(grad_q_low, "head", split_axis=1, concat_axis=2, tiled=True),
        lax.all_to_all(grad_k_low, "head", split_axis=1, concat_axis=2, tiled=True),
        lax.all_to_all(grad_v_low, "head", split_axis=1, concat_axis=2, tiled=True),
    )
    return (grad_query, grad_key, grad_value)


def solution(mesh):
    sections, nh, nb = (mesh.shape[a] for a in ("section", "head", "blk"))

    def per_device(query_states, key_states, value_states, grad_next, valid_count):
        lay = Layout(query_states.shape[1], query_states.shape[2], nb, nh)
        powers = nb & (nb - 1) == 0 and nh & (nh - 1) == 0 and nb > 1
        args = (query_states, key_states, value_states, grad_next, valid_count)
        if powers and lay.heads % nb == 0 and lay.part % 16 == 0:
            return split_heads_program(lay, *args, sections)
        return gathered_program(*args)

    return jax.shard_map(
        per_device,
        mesh=mesh,
        in_specs=(
            P("section", "blk", "head"),
            P("section", "blk", "head"),
            P("section", "blk", "head"),
            P("section", ("blk", "head"), None),
            P("section"),
        ),
        out_specs=(
            P("section", ("blk", "head"), None),
            P("section", ("blk", "head"), None),
            P("section", ("blk", "head"), None),
        ),
        check_vma=False,
    )
```
